32 devices in a mesh: frame: 8 (over z, y), audio: 4 (over x, core).
Axes of the slice: x: 2, y: 2, z: 4, core: 2. Of those that a mesh axis runs over, the one named last changes fastest.
Arguments:
- video: bfloat16 [25088, 768], P(('frame', 'audio')), may hold values from -6 to 6
- audio: bfloat16 [8192, 768], P(('frame', 'audio')), may hold values from -6 to 6
- w_query: bfloat16 [768, 768], replicated, may hold values from -9 to 9
- w_key: bfloat16 [768, 768], replicated, may hold values from -0.21875 to 0.21875
- w_value: bfloat16 [768, 768], replicated, may hold values from -0.21875 to 0.21875
- w_out: bfloat16 [768, 768], replicated, may hold values from -0.21875 to 0.21875
- grad_output: bfloat16 [25088, 768], P(('frame', 'audio')), may hold values from -6 to 6
- intersection_tiles: int32 [128, 8], P(('frame', 'audio')), may hold values from 0 to 63, as said below
- intersection_count: int32 [128], P(('frame', 'audio')), may hold values from 1 to 8
- tile_fill: int32 [64], P(('frame', 'audio')), may hold values from 32 to 128
Outputs:
- output: bfloat16 [25088, 768], P(('frame', 'audio'))
- grad_video: bfloat16 [25088, 768], P(('frame', 'audio'))
- grad_audio: bfloat16 [8192, 768], P(('frame', 'audio'))
- grad_w_query: float32 [768, 768], replicated
- grad_w_key: float32 [768, 768], replicated
- grad_w_value: float32 [768, 768], replicated
- grad_w_out: float32 [768, 768], replicated
The draws below stay inside these ranges and needn't reach their ends.
Inputs may be any that keep to these rules, and one draw needn't show every extreme that they name: `intersection_tiles`: entries j < intersection_count[f] of frame f are distinct tiles of index in [(f // 4 - 2) * 2, (f // 4 + 3) * 2); other entries are any tile.
All inputs are finite; a program needn't handle non-finite values.
Results may differ from the reference program's by a relative error of at most 0.0085.
The reference program's roundings to bfloat16 on the way count: a program that leaves them out, or rounds other values in their place, can miss the bound.
Values may be sent and summed in bfloat16 or wider, within the bound.
A program may use at most 192 MiB of HBM per device.

```python
import math
import jax
import jax.numpy as jnp
from jax import lax

D = 768
HEADS = 12
PATCH = 196
TILE = 128
REACH = 2
FR_DEV = 4
TILES_DEV = 2
LIST = 8
FRAMES = 128
TILES = 64
VTOK = 25088
SLOTS = 8192


def intersection_lists(key):
    window_tiles = (2 * REACH + 1) * TILES_DEV
    owner = jnp.arange(FRAMES, dtype=jnp.int32) // FR_DEV
    offsets = jnp.arange(window_tiles, dtype=jnp.int32)
    candidate = (owner[:, None] - REACH) * TILES_DEV + offsets[None, :]
    outside = ((candidate < 0) | (candidate >= TILES)).astype(jnp.int32)
    random_part = jax.random.randint(jax.random.fold_in(key, 11), (FRAMES, window_tiles), 0, 2 ** 20)
    ranking = outside * 2 ** 26 + random_part * window_tiles + offsets[None, :]
    ordering = jnp.argsort(ranking, axis=1)
    chosen = jnp.take_along_axis(candidate, ordering[:, :LIST], axis=1)
    chosen = jnp.clip(chosen, 0, TILES - 1).astype(jnp.int32)
    valid_count = window_tiles - jnp.sum(outside, axis=1)
    counts = jax.random.randint(jax.random.fold_in(key, 12), (FRAMES,), 1, LIST + 1)
    middle = FRAMES // 2
    counts = counts.at[middle].set(LIST).at[middle + 1].set(1)
    counts = jnp.minimum(counts, valid_count).astype(jnp.int32)
    return (chosen, counts)


def draw_intersection_tiles(key, part):
    chosen, counts = intersection_lists(key)
    return chosen


def draw_intersection_count(key, part):
    chosen, counts = intersection_lists(key)
    return counts


def draw_tile_fill(key, part):
    key = jax.random.fold_in(key, 3)
    filled = jax.random.randint(key, (TILES,), TILE // 4, TILE + 1)
    return filled.at[0].set(TILE).at[1].set(TILE // 4).astype(jnp.int32)


def draw_w_query(key, part):
    key = jax.random.fold_in(key, 5)
    matrix = jax.random.truncated_normal(key, -6.0, 6.0, (D, D), jnp.float32) * D ** (-0.5)
    return matrix.astype(jnp.bfloat16)


def steps_of(own_key, extent, shards, least, largest):
    level, own = 1.0, jax.random.fold_in(own_key, 6)
    for position, blocks in shards:
        steps = jnp.exp(jax.random.uniform(jax.random.fold_in(own, position), (blocks,), jnp.float32, least / len(shards), largest / len(shards)))
        level = level * jnp.repeat(steps, extent[position] // blocks).reshape([-1 if axis == position else 1 for axis in range(len(extent))])
    return level


def noise(key, dims, deviation, limit, split=(), kind=jnp.bfloat16):
    entries = deviation * jax.random.normal(key, dims, jnp.float32)
    if split:
        entries = entries * steps_of(key, dims, split, -0.22, 0.18)
    return jnp.clip(entries, -limit, limit).astype(kind)


def setup_inputs(seed: int = 0) -> dict:
    key_of = jax.random.split(jax.random.key(seed), 11)
    return {
        "video": noise(key_of[0], (VTOK, D), 1.0, 6.0, ((0, 32),)),
        "audio": noise(key_of[1], (SLOTS, D), 1.0, 6.0, ((0, 32),)),
        "w_query": draw_w_query(jax.random.fold_in(key_of[10], 71), 0),
        "w_key": noise(key_of[3], (D, D), D ** -0.5, 0.21875),
        "w_value": noise(key_of[4], (D, D), D ** -0.5, 0.21875),
        "w_out": noise(key_of[5], (D, D), D ** -0.5, 0.21875),
        "grad_output": noise(key_of[6], (VTOK, D), 1.0, 6.0, ((0, 32),)),
        "intersection_tiles": draw_intersection_tiles(jax.random.fold_in(key_of[10], 71), 0),
        "intersection_count": draw_intersection_count(jax.random.fold_in(key_of[10], 71), 0),
        "tile_fill": draw_tile_fill(jax.random.fold_in(key_of[10], 71), 0),
    }


def normalize(row_block):
    centred = row_block.astype(jnp.float32)
    centred = centred - lax.optimization_barrier(jnp.mean(centred, axis=-1, keepdims=True))
    inverse = lax.rsqrt(lax.optimization_barrier(jnp.mean(centred * centred, axis=-1, keepdims=True)) + 1e-05)
    normed_hat = centred * inverse
    return (normed_hat.astype(jnp.bfloat16), normed_hat, inverse)

def normalize_back(gradient, normed_hat, inverse):
    first = lax.optimization_barrier(jnp.mean(gradient, axis=-1, keepdims=True))
    second = lax.optimization_barrier(jnp.mean(gradient * normed_hat, axis=-1, keepdims=True))
    return inverse * (gradient - first - normed_hat * second)

def frame_step(query_frame, dcontext_frame, key_window, value_window, filled_window, local_tile, used_count):
    features = query_frame.shape[1]
    head_size = features // HEADS
    score_scale = 1.0 / math.sqrt(head_size)
    chosen_keys = key_window[local_tile].reshape(-1, HEADS, head_size).astype(jnp.float32)
    chosen_values = value_window[local_tile].reshape(-1, HEADS, head_size).astype(jnp.float32)
    listed = (jnp.arange(local_tile.shape[0]) < used_count).astype(jnp.float32)
    visible = (filled_window[local_tile] * listed[:, None]).reshape(-1)
    queries = query_frame.reshape(-1, HEADS, head_size).astype(jnp.float32)
    dcontext = dcontext_frame.reshape(-1, HEADS, head_size).astype(jnp.float32)
    scores = jnp.einsum('phd,khd->hpk', queries, chosen_keys) * score_scale
    scores = jnp.where(visible > 0, scores, -1e+30)
    highest = lax.optimization_barrier(jnp.max(scores, axis=-1, keepdims=True))
    exponent = jnp.exp(scores - highest) * visible
    attention = exponent / lax.optimization_barrier(jnp.sum(exponent, axis=-1, keepdims=True))
    attention_low = attention.astype(jnp.bfloat16).astype(jnp.float32)
    context = jnp.einsum('hpk,khd->phd', attention_low, chosen_values).astype(jnp.bfloat16).reshape(-1, features)
    dattention = jnp.einsum('phd,khd->hpk', dcontext, chosen_values)
    dscores = attention * (dattention - lax.optimization_barrier(jnp.sum(attention * dattention, axis=-1, keepdims=True))) * score_scale
    dscores = dscores.astype(jnp.bfloat16).astype(jnp.float32)
    dquery = jnp.einsum('hpk,khd->phd', dscores, chosen_keys).astype(jnp.bfloat16).reshape(-1, features)
    dkeys = jnp.einsum('hpk,phd->khd', dscores, queries).reshape(local_tile.shape[0], -1, features)
    dvalues = jnp.einsum('hpk,phd->khd', attention_low, dcontext).reshape(local_tile.shape[0], -1, features)
    return (context, dquery, dkeys, dvalues)

def block_step(query_block, dcontext_block, key_window, value_window, filled_window, local_block, count_block):
    empty = jnp.zeros(key_window.shape, jnp.float32)

    def per_frame(running, inputs_now):
        query_frame, dcontext_frame, local_tile, used_count = inputs_now
        context, dquery, dkeys, dvalues = frame_step(query_frame, dcontext_frame, key_window, value_window, filled_window, local_tile, used_count)
        return ((running[0].at[local_tile].add(dkeys), running[1].at[local_tile].add(dvalues)), (context, dquery))
    (summed_keys, summed_values), (context, dquery) = lax.scan(per_frame, (empty, empty), (query_block, dcontext_block, local_block, count_block))
    return (context, dquery, summed_keys.astype(jnp.bfloat16), summed_values.astype(jnp.bfloat16))

def reference(video, audio, w_query, w_key, w_value, w_out, grad_output, intersection_tiles, intersection_count, tile_fill):
    video_normed, video_hat, video_inverse = normalize(video)
    audio_normed, audio_hat, audio_inverse = normalize(audio)
    query = jnp.dot(video_normed, w_query, preferred_element_type=jnp.float32).astype(jnp.bfloat16)
    key_rows = jnp.dot(audio_normed, w_key, preferred_element_type=jnp.float32).astype(jnp.bfloat16)
    values = jnp.dot(audio_normed, w_value, preferred_element_type=jnp.float32).astype(jnp.bfloat16)
    dcontext = jnp.dot(grad_output, w_out.T, preferred_element_type=jnp.float32).astype(jnp.bfloat16)
    blocks = FRAMES // FR_DEV
    margin_tiles = REACH * TILES_DEV
    window_tiles = (2 * REACH + 1) * TILES_DEV
    padding = ((margin_tiles, margin_tiles), (0, 0), (0, 0))
    key_tiles = jnp.pad(key_rows.reshape(TILES, TILE, D), padding)
    value_tiles = jnp.pad(values.reshape(TILES, TILE, D), padding)
    filled = (jnp.arange(TILE)[None, :] < tile_fill[:, None]).astype(jnp.float32)
    filled = jnp.pad(filled, ((margin_tiles, margin_tiles), (0, 0)))
    query_blocks = query.reshape(blocks, FR_DEV, PATCH, D)
    dcontext_blocks = dcontext.reshape(blocks, FR_DEV, PATCH, D)
    list_blocks = intersection_tiles.reshape(blocks, FR_DEV, LIST)
    count_blocks = intersection_count.reshape(blocks, FR_DEV)
    empty = jnp.zeros(key_tiles.shape, jnp.float32)

    def per_block(running, inputs_now):
        block_number, query_block, dcontext_block, list_block, count_block = inputs_now
        first_tile = (block_number * TILES_DEV).astype(jnp.int32)
        key_window = lax.dynamic_slice_in_dim(key_tiles, first_tile, window_tiles, 0)
        value_window = lax.dynamic_slice_in_dim(value_tiles, first_tile, window_tiles, 0)
        filled_window = lax.dynamic_slice_in_dim(filled, first_tile, window_tiles, 0)
        local_block = jnp.clip(list_block - (block_number - REACH) * TILES_DEV, 0, window_tiles - 1).astype(jnp.int32)
        context, dquery, dkeys, dvalues = block_step(query_block, dcontext_block, key_window, value_window, filled_window, local_block, count_block)
        summed_keys = lax.dynamic_slice_in_dim(running[0], first_tile, window_tiles, 0) + dkeys.astype(jnp.float32)
        summed_values = lax.dynamic_slice_in_dim(running[1], first_tile, window_tiles, 0) + dvalues.astype(jnp.float32)
        new_keys = lax.dynamic_update_slice_in_dim(running[0], summed_keys, first_tile, 0)
        new_values = lax.dynamic_update_slice_in_dim(running[1], summed_values, first_tile, 0)
        return ((new_keys, new_values), (context, dquery))
    inputs_all = (jnp.arange(blocks, dtype=jnp.int32), query_blocks, dcontext_blocks, list_blocks, count_blocks)
    (key_grads, value_grads), (context, dquery) = lax.scan(per_block, (empty, empty), inputs_all)
    dkeys = key_grads[margin_tiles:margin_tiles + TILES].reshape(SLOTS, D)
    dvalues = value_grads[margin_tiles:margin_tiles + TILES].reshape(SLOTS, D)
    context = context.reshape(VTOK, D)
    dquery = dquery.reshape(VTOK, D)
    attended = jnp.dot(context, w_out, preferred_element_type=jnp.float32)
    output = (video.astype(jnp.float32) + attended).astype(jnp.bfloat16)
    grad_w_out = jnp.dot(context.T, grad_output, preferred_element_type=jnp.float32)
    grad_w_query = jnp.dot(video_normed.T, dquery, preferred_element_type=jnp.float32)
    dvideo_normed = jnp.dot(dquery, w_query.T, preferred_element_type=jnp.float32)
    grad_video = (grad_output.astype(jnp.float32) + normalize_back(dvideo_normed, video_hat, video_inverse)).astype(jnp.bfloat16)
    highest = lax.Precision.HIGHEST
    daudio_normed = jnp.dot(dkeys, w_key.astype(jnp.float32).T, precision=highest) + jnp.dot(dvalues, w_value.astype(jnp.float32).T, precision=highest)
    grad_audio = normalize_back(daudio_normed, audio_hat, audio_inverse).astype(jnp.bfloat16)
    audio_wide = audio_normed.astype(jnp.float32).T
    grad_w_key = jnp.dot(audio_wide, dkeys, precision=highest)
    grad_w_value = jnp.dot(audio_wide, dvalues, precision=highest)
    return (output, grad_video, grad_audio, grad_w_query, grad_w_key, grad_w_value, grad_w_out)
```

```python
import functools
import math

import jax
import jax.numpy as jnp
from jax import lax
from jax.experimental import pallas as pl
from jax.experimental.pallas import tpu as pltpu
from jax.sharding import PartitionSpec as P

HEADS = 12
TILE = 128
REACH = 2
GROUPS = 3
SIZES = (2, 4, 6, 8)


def shifted(block, axis, distance):
    devices = range(lax.axis_size(axis))
    route = [(i - distance, i) for i in devices if i - distance in devices]
    return lax.ppermute(block, axis, route)


def normalize(row_block):
    centred = row_block.astype(jnp.float32)
    centred = centred - jnp.mean(centred, axis=-1, keepdims=True)
    inverse = lax.rsqrt(jnp.mean(centred * centred, axis=-1, keepdims=True) + 1e-05)
    normed_hat = centred * inverse
    return (normed_hat.astype(jnp.bfloat16), normed_hat, inverse)


def normalize_back(gradient, normed_hat, inverse):
    first = jnp.mean(gradient, axis=-1, keepdims=True)
    second = jnp.mean(gradient * normed_hat, axis=-1, keepdims=True)
    return inverse * (gradient - first - normed_hat * second)


def dot_nt(left, right):
    return lax.dot_general(left, right, (((1,), (1,)), ((), ())), preferred_element_type=jnp.float32)


def dot_nn(left, right):
    return jnp.dot(left, right, preferred_element_type=jnp.float32)


def per_head(reduced, low, high):
    rows = low.shape[0]
    return jnp.concatenate(
        [
            jnp.broadcast_to(reduced(low, axis=1, keepdims=True), (rows, TILE)),
            jnp.broadcast_to(reduced(high, axis=1, keepdims=True), (rows, TILE)),
        ],
        axis=1,
    )


def attention_kernel(
    tiles_ref,
    count_ref,
    fill_ref,
    query_ref,
    dcontext_ref,
    keys_ref,
    values_ref,
    context_ref,
    dquery_ref,
    dkeys_ref,
    dvalues_ref,
    pair_keys,
    pair_values,
    sum_keys,
    sum_values,
    query_pad,
    dcontext_pad,
    scores_scr,
    dattention_scr,
    low_scr,
    dscores_scr,
):
    frame = pl.program_id(1)
    patch = query_ref.shape[1]
    padded, width = query_pad.shape
    half = width // 2
    listed = tiles_ref.shape[1]
    window = pair_keys.shape[0]
    scale = 1.0 / math.sqrt(half)

    @pl.when(frame == 0)
    def _():
        first = lax.broadcasted_iota(jnp.int32, (TILE, width), 1) < half
        for tile in range(window):
            for source, target in ((keys_ref, pair_keys), (values_ref, pair_values)):
                block = source[tile * TILE : (tile + 1) * TILE, :]
                zero = jnp.zeros_like(block)
                target[tile, :TILE, :] = jnp.where(first, block, zero)
                target[tile, TILE:, :] = jnp.where(first, zero, block)
        sum_keys[...] = jnp.zeros_like(sum_keys)
        sum_values[...] = jnp.zeros_like(sum_values)
        for pad in (query_pad, dcontext_pad):
            pad[padded - 16 :, :] = jnp.zeros((16, width), pad.dtype)

    query_pad[:patch, :] = query_ref[0] * jnp.asarray(scale, query_ref.dtype)
    dcontext_pad[:patch, :] = dcontext_ref[0]
    count = count_ref[frame]

    def work(slots):
        query = query_pad[...]
        dcontext = dcontext_pad[...]
        query_t = query.T
        dcontext_t = dcontext.T
        lane = lax.rem(lax.broadcasted_iota(jnp.int32, (1, 2 * TILE), 1), TILE)
        places, biases = [], []
        for j in range(slots):
            place = tiles_ref[frame, j]
            seen = jnp.where(j < count, fill_ref[place], 0)
            places.append(place)
            biases.append(jnp.where(lane < seen, 0.0, -1e30))
        for j in range(slots):
            columns = slice(j * 2 * TILE, (j + 1) * 2 * TILE)
            scores_scr[:, columns] = dot_nt(query, pair_keys[places[j]]) + biases[j]
            dattention_scr[:, columns] = dot_nt(dcontext, pair_values[places[j]])
        for start in range(0, padded, 16):
            rows = slice(start, start + 16)
            scores = [scores_scr[rows, j * 2 * TILE : (j + 1) * 2 * TILE] for j in range(slots)]
            highest = functools.reduce(jnp.maximum, scores)
            highest = per_head(jnp.max, highest[:, :TILE], highest[:, TILE:])
            exponent = [jnp.exp(part - highest) for part in scores]
            total = functools.reduce(jnp.add, exponent)
            inverse = 1.0 / per_head(jnp.sum, total[:, :TILE], total[:, TILE:])
            attention = [part * inverse for part in exponent]
            dattention = [
                dattention_scr[rows, j * 2 * TILE : (j + 1) * 2 * TILE] for j in range(slots)
            ]
            weighed = functools.reduce(
                jnp.add, [a * b for a, b in zip(attention, dattention)]
            )
            weighed = per_head(jnp.sum, weighed[:, :TILE], weighed[:, TILE:])
            for j in range(slots):
                columns = slice(j * 2 * TILE, (j + 1) * 2 * TILE)
                low_scr[rows, columns] = attention[j].astype(jnp.bfloat16)
                dscores_scr[rows, columns] = (
                    attention[j] * (dattention[j] - weighed)
                ).astype(jnp.bfloat16)
        context = jnp.zeros((padded, width), jnp.float32)
        dquery = jnp.zeros((padded, width), jnp.float32)
        for j in range(slots):
            columns = slice(j * 2 * TILE, (j + 1) * 2 * TILE)
            low, dscores = low_scr[:, columns], dscores_scr[:, columns]
            context += dot_nn(low, pair_values[places[j]])
            dquery += dot_nn(dscores, pair_keys[places[j]])
            sum_keys[places[j]] += dot_nn(query_t, dscores)
            sum_values[places[j]] += dot_nn(dcontext_t, low)
        context_ref[0] = context[:patch].astype(context_ref.dtype)
        dquery_ref[0] = (dquery[:patch] * scale).astype(dquery_ref.dtype)

    least = 0
    for slots in sorted({min(size, listed) for size in SIZES} | {listed}):
        pl.when((count > least) & (count <= slots))(functools.partial(work, slots))
        least = slots

    @pl.when(frame == pl.num_programs(1) - 1)
    def _():
        for total, target in ((sum_keys, dkeys_ref), (sum_values, dvalues_ref)):
            for tile in range(window):
                columns = slice(tile * TILE, (tile + 1) * TILE)
                target[:half, columns] = total[tile, :half, :TILE].astype(target.dtype)
                target[half:, columns] = total[tile, half:, TILE:].astype(target.dtype)


def attend(local_block, count_block, fill_window, query, dcontext, key_window, value_window):
    frames, patch, width = query.shape
    slots = key_window.shape[0]
    window = slots // TILE
    listed = local_block.shape[1]
    pair = 2 * TILE // 2
    padded = -(-patch // 16) * 16
    frame_spec = pl.BlockSpec((1, patch, pair), lambda p, f, *_: (f, 0, p))
    window_spec = pl.BlockSpec((slots, pair), lambda p, f, *_: (0, p))
    sums_spec = pl.BlockSpec((pair, slots), lambda p, f, *_: (p, 0))
    work = frames * patch * width * listed * TILE
    return pl.pallas_call(
        attention_kernel,
        grid_spec=pltpu.PrefetchScalarGridSpec(
            num_scalar_prefetch=3,
            grid=(width // pair, frames),
            in_specs=[frame_spec, frame_spec, window_spec, window_spec],
            out_specs=[frame_spec, frame_spec, sums_spec, sums_spec],
            scratch_shapes=[
                pltpu.VMEM((window, 2 * TILE, pair), jnp.bfloat16),
                pltpu.VMEM((window, 2 * TILE, pair), jnp.bfloat16),
                pltpu.VMEM((window, pair, 2 * TILE), jnp.float32),
                pltpu.VMEM((window, pair, 2 * TILE), jnp.float32),
                pltpu.VMEM((padded, pair), jnp.bfloat16),
                pltpu.VMEM((padded, pair), jnp.bfloat16),
                pltpu.VMEM((padded, listed * 2 * TILE), jnp.float32),
                pltpu.VMEM((padded, listed * 2 * TILE), jnp.float32),
                pltpu.VMEM((padded, listed * 2 * TILE), jnp.bfloat16),
                pltpu.VMEM((padded, listed * 2 * TILE), jnp.bfloat16),
            ],
        ),
        out_shape=[
            jax.ShapeDtypeStruct(query.shape, jnp.bfloat16),
            jax.ShapeDtypeStruct(query.shape, jnp.bfloat16),
            jax.ShapeDtypeStruct((width, slots), jnp.bfloat16),
            jax.ShapeDtypeStruct((width, slots), jnp.bfloat16),
        ],
        compiler_params=pltpu.CompilerParams(vmem_limit_bytes=40 * 1024 * 1024),
        cost_estimate=pl.CostEstimate(
            flops=48 * work,
            bytes_accessed=8 * frames * patch * width + 8 * slots * width,
            transcendentals=work // 64,
        ),
        name="attend",
    )(local_block, count_block, fill_window, query, dcontext, key_window, value_window)


def per_device(
    video,
    audio,
    w_query,
    w_key,
    w_value,
    w_out,
    grad_output,
    intersection_tiles,
    intersection_count,
    tile_fill,
):
    tiles_dev = tile_fill.shape[0]
    window_tiles = (2 * REACH + 1) * tiles_dev
    frames = intersection_count.shape[0]
    features = video.shape[1]
    contract_rows = (((0,), (0,)), ((), ()))
    video_normed, video_hat, video_inverse = normalize(video)
    audio_normed, audio_hat, audio_inverse = normalize(audio)
    device_index = lax.axis_index(("frame", "audio"))
    normed_tiles = audio_normed.reshape(tiles_dev, TILE, features)
    normed_parts, fill_parts = ([], [])
    for offset in range(-REACH, REACH + 1):
        if offset == 0:
            received = (normed_tiles, tile_fill)
        else:
            received = shifted((normed_tiles, tile_fill), ("frame", "audio"), -offset)
        normed_parts.append(received[0])
        fill_parts.append(received[1])
    normed_window = jnp.concatenate(normed_parts, axis=0).reshape(-1, features)
    fill_window = jnp.concatenate(fill_parts, axis=0)
    local_block = jnp.clip(
        intersection_tiles - (device_index - REACH) * tiles_dev, 0, window_tiles - 1
    )
    group = features // GROUPS
    contexts, dqueries, dkeys, dvalues, sums = ([], [], [], [], [])
    for first in range(0, features, group):
        part = slice(first, first + group)
        query = dot_nn(video_normed, w_query[:, part]).astype(jnp.bfloat16)
        dcontext = dot_nt(grad_output, w_out[part]).astype(jnp.bfloat16)
        key_window = dot_nn(normed_window, w_key[:, part]).astype(jnp.bfloat16)
        value_window = dot_nn(normed_window, w_value[:, part]).astype(jnp.bfloat16)
        context, dquery, dkeys_t, dvalues_t = attend(
            local_block,
            intersection_count,
            fill_window,
            query.reshape(frames, -1, group),
            dcontext.reshape(frames, -1, group),
            key_window,
            value_window,
        )
        context = context.reshape(-1, group)
        dquery = dquery.reshape(-1, group)
        contexts.append(context)
        dqueries.append(dquery)
        dkeys.append(dkeys_t)
        dvalues.append(dvalues_t)
        window_rows = (((0,), (1,)), ((), ()))
        partial_sums = (
            lax.dot_general(
                video_normed, dquery, contract_rows, preferred_element_type=jnp.float32
            ),
            lax.dot_general(
                normed_window, dkeys_t, window_rows, preferred_element_type=jnp.float32
            ),
            lax.dot_general(
                normed_window, dvalues_t, window_rows, preferred_element_type=jnp.float32
            ),
            lax.dot_general(
                grad_output, context, contract_rows, preferred_element_type=jnp.float32
            ),
        )
        if sums:
            partial_sums, sums[-1] = lax.optimization_barrier((partial_sums, sums[-1]))
        sums.append(lax.psum(partial_sums, ("frame", "audio")))
    dkeys = jnp.concatenate(dkeys, axis=0)
    dvalues = jnp.concatenate(dvalues, axis=0)
    context = jnp.concatenate(contexts, axis=1)
    dquery = jnp.concatenate(dqueries, axis=1)
    rows_cols = (((0,), (1,)), ((), ()))
    dnormed_window = lax.dot_general(dkeys, w_key, rows_cols, preferred_element_type=jnp.float32)
    dnormed_window = dnormed_window + lax.dot_general(
        dvalues, w_value, rows_cols, preferred_element_type=jnp.float32
    )
    dnormed_window = dnormed_window.reshape(window_tiles, TILE, features)
    own_first = REACH * tiles_dev
    daudio_normed = dnormed_window[own_first : own_first + tiles_dev]
    for offset in range(-REACH, REACH + 1):
        if offset != 0:
            first_tile = (offset + REACH) * tiles_dev
            returned = shifted(
                dnormed_window[first_tile : first_tile + tiles_dev], ("frame", "audio"), offset
            )
            daudio_normed = daudio_normed + returned
    daudio_normed = daudio_normed.reshape(-1, features)
    grad_audio = normalize_back(daudio_normed, audio_hat, audio_inverse).astype(jnp.bfloat16)
    attended = dot_nn(context, w_out)
    output = (video.astype(jnp.float32) + attended).astype(jnp.bfloat16)
    dvideo_normed = dot_nt(dquery, w_query)
    grad_video = (
        grad_output.astype(jnp.float32) + normalize_back(dvideo_normed, video_hat, video_inverse)
    ).astype(jnp.bfloat16)
    grad_query, grad_key, grad_value = (
        jnp.concatenate([total[i] for total in sums], axis=1) for i in range(3)
    )
    grad_out = jnp.concatenate([total[3].T for total in sums], axis=0)
    return (output, grad_video, grad_audio, grad_query, grad_key, grad_value, grad_out)


def solution(mesh):
    in_specs = (
        P(("frame", "audio"), None),
        P(("frame", "audio"), None),
        P(),
        P(),
        P(),
        P(),
        P(("frame", "audio"), None),
        P(("frame", "audio"), None),
        P(("frame", "audio")),
        P(("frame", "audio")),
    )
    out_specs = (
        P(("frame", "audio"), None),
        P(("frame", "audio"), None),
        P(("frame", "audio"), None),
        P(),
        P(),
        P(),
        P(),
    )
    return jax.shard_map(
        per_device, mesh=mesh, in_specs=in_specs, out_specs=out_specs, check_vma=False
    )
```

```python
import functools
import math

import jax
import jax.numpy as jnp
from jax import lax
from jax.experimental import pallas as pl
from jax.experimental.pallas import tpu as pltpu
from jax.sharding import PartitionSpec as P

HEADS = 12
TILE = 128
REACH = 2
STREAMS = 3
LANES = 384
WIRE = jnp.bfloat16
MESH = pl.DeviceIdType.MESH
SIZES = (2, 4, 6, 8)


def neighbour(distance):
    inner, total = lax.axis_size("audio"), lax.axis_size("audio") * lax.axis_size("frame")
    index = lax.axis_index("frame") * inner + lax.axis_index("audio") + distance
    exists = (index >= 0) & (index < total)
    index = lax.rem(index + total, total)
    return (index // inner, lax.rem(index, inner)), exists


def other_offsets():
    return [offset for offset in range(-REACH, REACH + 1) if offset != 0]


def greet_neighbours(barrier, others=0):
    for offset in other_offsets():
        device, _ = neighbour(offset)
        pl.semaphore_signal(barrier, inc=1, device_id=device, device_id_type=MESH)
    pl.semaphore_wait(barrier, 2 * REACH + others)


def halo_kernel(rows_ref, fill_ref, window_ref, fills_ref, send_sems, recv_sems):
    greet_neighbours(pltpu.get_barrier_semaphore())

    def copies(offset):
        device, exists = neighbour(offset)
        place = REACH - offset
        return exists, [
            pltpu.make_async_remote_copy(
                src_ref=source,
                dst_ref=target.at[place],
                send_sem=send_sems.at[i, place],
                recv_sem=recv_sems.at[i, place],
                device_id=device,
                device_id_type=MESH,
            )
            for i, (source, target) in enumerate(((rows_ref, window_ref), (fill_ref, fills_ref)))
        ]

    for offset in other_offsets():
        exists, pair = copies(offset)

        @pl.when(exists)
        def _():
            for copy in pair:
                copy.start()

    window_ref[REACH] = rows_ref[...]
    fills_ref[REACH] = fill_ref[...]
    for offset in other_offsets():
        _, exists = neighbour(-offset)
        place = REACH - offset

        @pl.when(jnp.logical_not(exists))
        def _():
            window_ref[place] = jnp.zeros(rows_ref.shape, rows_ref.dtype)
            fills_ref[place] = jnp.zeros(fill_ref.shape, fill_ref.dtype)

    for offset in other_offsets():
        exists, pair = copies(offset)
        _, comes = neighbour(-offset)

        @pl.when(exists)
        def _():
            for copy in pair:
                copy.wait_send()

        @pl.when(comes)
        def _():
            for copy in pair:
                copy.wait_recv()


def gather_halo(rows, fill):
    vmem = pl.BlockSpec(memory_space=pltpu.VMEM)
    spread = 2 * REACH + 1
    return pl.pallas_call(
        halo_kernel,
        in_specs=[vmem, vmem],
        out_specs=[vmem, vmem],
        out_shape=[
            jax.ShapeDtypeStruct((spread, *rows.shape), rows.dtype),
            jax.ShapeDtypeStruct((spread, *fill.shape), fill.dtype),
        ],
        scratch_shapes=[
            pltpu.SemaphoreType.DMA((2, spread)),
            pltpu.SemaphoreType.DMA((2, spread)),
        ],
        compiler_params=pltpu.CompilerParams(
            collective_id=1, has_side_effects=True, vmem_limit_bytes=16 * 1024 * 1024
        ),
        name="gather_halo",
    )(rows, fill)


def partner(axis, bit):
    me = lax.axis_index(axis)
    mine = lax.rem(me // (1 << bit), 2)
    other = me + (1 << bit) * (1 - 2 * mine)
    if axis == "frame":
        return (other, lax.axis_index("audio")), mine
    return (lax.axis_index("frame"), other), mine


def sum_kernel(
    bits,
    sums_ref,
    back_ref,
    total_ref,
    returned_ref,
    whole_recv,
    running,
    outgoing,
    incoming,
    send_sems,
    recv_sems,
    gather_send,
    gather_recv,
    back_send,
    back_recv,
):
    steps = len(bits)
    depth = total_ref.shape[0] // STREAMS
    middle = list(bits[1:-1])
    orders = []
    for stream in range(STREAMS):
        turn = stream % len(middle)
        orders.append([bits[0], *middle[turn:], *middle[:turn], bits[-1]])
    barrier = pltpu.get_barrier_semaphore()
    for axis, bit in bits:
        device, _ = partner(axis, bit)
        pl.semaphore_signal(barrier, inc=1, device_id=device, device_id_type=MESH)
    greet_neighbours(barrier, steps)

    def remote(source, target, send_sem, recv_sem, device):
        return pltpu.make_async_remote_copy(
            src_ref=source,
            dst_ref=target,
            send_sem=send_sem,
            recv_sem=recv_sem,
            device_id=device,
            device_id_type=MESH,
        )

    def aligned(row):
        return pl.multiple_of(row, 16)

    def by_rows(rows, body):
        chunk = min(rows, 64)

        def step(i, carry):
            body(i * chunk, chunk)
            return carry

        lax.fori_loop(0, rows // chunk, step, 0)

    bases = [0] * STREAMS
    started = []

    def start_step(stream, k):
        device, mine = partner(*orders[stream][k])
        rows = depth >> (k + 1)
        semaphores = (send_sems.at[stream, k], recv_sems.at[stream, k])
        if k == 0:
            away = aligned(stream * depth + (1 - mine) * rows)
            copy = remote(sums_ref.at[pl.ds(away, rows)], whole_recv.at[stream], *semaphores, device)
        else:
            away = bases[stream] + (1 - mine) * rows

            def cast(i, chunk):
                at = pl.ds(aligned(away + i), chunk)
                outgoing[stream, at, :] = running[stream, at, :].astype(outgoing.dtype)

            by_rows(rows, cast)
            place = depth // 2 - 2 * rows
            copy = remote(
                outgoing.at[stream, pl.ds(aligned(away), rows)],
                incoming.at[stream, pl.ds(place, rows)],
                *semaphores,
                device,
            )
        copy.start()
        return copy

    def finish_step(stream, k, copy):
        _, mine = partner(*orders[stream][k])
        rows = depth >> (k + 1)
        copy.wait_recv()
        if k == 0:
            kept = stream * depth + mine * rows

            def add(i, chunk):
                at = pl.ds(pl.multiple_of(i, 16), chunk)
                own = sums_ref[pl.ds(aligned(kept + i), chunk), :]
                running[stream, at, :] = own + whole_recv[stream, at, :]

        else:
            bases[stream] = bases[stream] + mine * rows
            place = depth // 2 - 2 * rows

            def add(i, chunk):
                at = pl.ds(aligned(bases[stream] + i), chunk)
                arrived = incoming[stream, pl.ds(aligned(place + i), chunk), :]
                running[stream, at, :] += arrived.astype(running.dtype)

        by_rows(rows, add)

    live = [start_step(stream, 0) for stream in range(STREAMS)]

    def back_copy(offset):
        device, exists = neighbour(offset)
        place = offset + REACH - (offset > 0)
        return exists, remote(
            back_ref.at[place], returned_ref.at[place], back_send.at[place], back_recv.at[place], device
        )

    for offset in other_offsets():
        exists, copy = back_copy(offset)
        pl.when(exists)(copy.start)
    for offset in other_offsets():
        _, comes = neighbour(-offset)
        place = offset + REACH - (offset > 0)

        @pl.when(jnp.logical_not(comes))
        def _():
            returned_ref[place] = jnp.zeros(returned_ref.shape[1:], returned_ref.dtype)

    for k in range(steps):
        for stream in range(STREAMS):
            finish_step(stream, k, live[stream])
            started.append(live[stream])
            if k + 1 < steps:
                live[stream] = start_step(stream, k + 1)

    def gather_copy(stream, k, first):
        device, _ = partner(*orders[stream][k])
        at = pl.ds(aligned(first), depth >> (k + 1))
        return remote(
            total_ref.at[at], total_ref.at[at], gather_send.at[stream, k], gather_recv.at[stream, k], device
        )

    firsts = []
    for stream in range(STREAMS):
        _, mine = partner(*orders[stream][0])
        first = stream * depth + mine * (depth // 2) + bases[stream]
        rows = depth >> steps

        def finish(i, chunk):
            own = running[stream, pl.ds(aligned(bases[stream] + i), chunk), :]
            total_ref[pl.ds(aligned(first + i), chunk), :] = own.astype(total_ref.dtype)

        by_rows(rows, finish)
        firsts.append(first)
        live[stream] = gather_copy(stream, steps - 1, first)
        live[stream].start()
    for k in reversed(range(steps)):
        for stream in range(STREAMS):
            _, mine = partner(*orders[stream][k])
            live[stream].wait_recv()
            started.append(live[stream])
            firsts[stream] = firsts[stream] - mine * (depth >> (k + 1))
            if k > 0:
                live[stream] = gather_copy(stream, k - 1, firsts[stream])
                live[stream].start()
    for copy in started:
        copy.wait_send()
    for offset in other_offsets():
        exists, copy = back_copy(offset)
        _, comes = neighbour(-offset)
        pl.when(exists)(copy.wait_send)
        pl.when(comes)(copy.wait_recv)


def sum_devices(sums, back):
    bits = [
        (axis, bit)
        for axis in ("audio", "frame")
        for bit in range((lax.axis_size(axis) - 1).bit_length())
    ]
    steps = len(bits)
    depth = sums.shape[0] // STREAMS
    vmem = pl.BlockSpec(memory_space=pltpu.VMEM)
    return pl.pallas_call(
        functools.partial(sum_kernel, bits),
        in_specs=[vmem, vmem],
        out_specs=[vmem, vmem],
        out_shape=[
            jax.ShapeDtypeStruct(sums.shape, jnp.bfloat16),
            jax.ShapeDtypeStruct(back.shape, back.dtype),
        ],
        scratch_shapes=[
            pltpu.VMEM((STREAMS, depth // 2, sums.shape[1]), jnp.float32),
            pltpu.VMEM((STREAMS, depth // 2, sums.shape[1]), jnp.float32),
            pltpu.VMEM((STREAMS, depth // 2, sums.shape[1]), WIRE),
            pltpu.VMEM((STREAMS, depth // 2, sums.shape[1]), WIRE),
            pltpu.SemaphoreType.DMA((STREAMS, steps)),
            pltpu.SemaphoreType.DMA((STREAMS, steps)),
            pltpu.SemaphoreType.DMA((STREAMS, steps)),
            pltpu.SemaphoreType.DMA((STREAMS, steps)),
            pltpu.SemaphoreType.DMA((2 * REACH,)),
            pltpu.SemaphoreType.DMA((2 * REACH,)),
        ],
        compiler_params=pltpu.CompilerParams(
            collective_id=2, has_side_effects=True, vmem_limit_bytes=48 * 1024 * 1024
        ),
        name="sum_devices",
    )(sums, back)


def normalize(row_block):
    centred = row_block.astype(jnp.float32)
    centred = centred - jnp.mean(centred, axis=-1, keepdims=True)
    inverse = lax.rsqrt(jnp.mean(centred * centred, axis=-1, keepdims=True) + 1e-05)
    normed_hat = centred * inverse
    return (normed_hat.astype(jnp.bfloat16), normed_hat, inverse)


def normalize_back(gradient, normed_hat, inverse):
    first = jnp.mean(gradient, axis=-1, keepdims=True)
    second = jnp.mean(gradient * normed_hat, axis=-1, keepdims=True)
    return inverse * (gradient - first - normed_hat * second)


def dot_nt(left, right):
    return lax.dot_general(left, right, (((1,), (1,)), ((), ())), preferred_element_type=jnp.float32)


def dot_nn(left, right):
    return jnp.dot(left, right, preferred_element_type=jnp.float32)


def per_head(reduced, low, high):
    rows = low.shape[0]
    return jnp.concatenate(
        [
            jnp.broadcast_to(reduced(low, axis=1, keepdims=True), (rows, TILE)),
            jnp.broadcast_to(reduced(high, axis=1, keepdims=True), (rows, TILE)),
        ],
        axis=1,
    )


def attention_kernel(
    tiles_ref,
    count_ref,
    fill_ref,
    query_ref,
    dcontext_ref,
    keys_ref,
    values_ref,
    context_ref,
    dquery_ref,
    dkeys_ref,
    dvalues_ref,
    pair_keys,
    pair_values,
    sum_keys,
    sum_values,
    query_pad,
    dcontext_pad,
    scores_scr,
    dattention_scr,
    low_scr,
    dscores_scr,
):
    frame = pl.program_id(1)
    patch = query_ref.shape[1]
    padded, width = query_pad.shape
    half = width // 2
    listed = tiles_ref.shape[1]
    window = pair_keys.shape[0]
    scale = 1.0 / math.sqrt(half)

    @pl.when(frame == 0)
    def _():
        first = lax.broadcasted_iota(jnp.int32, (TILE, width), 1) < half
        for tile in range(window):
            for source, target in ((keys_ref, pair_keys), (values_ref, pair_values)):
                block = source[tile * TILE : (tile + 1) * TILE, :]
                zero = jnp.zeros_like(block)
                target[tile, :TILE, :] = jnp.where(first, block, zero)
                target[tile, TILE:, :] = jnp.where(first, zero, block)
        sum_keys[...] = jnp.zeros_like(sum_keys)
        sum_values[...] = jnp.zeros_like(sum_values)
        for pad in (query_pad, dcontext_pad):
            pad[padded - 16 :, :] = jnp.zeros((16, width), pad.dtype)

    query_pad[:patch, :] = query_ref[0] * jnp.asarray(scale, query_ref.dtype)
    dcontext_pad[:patch, :] = dcontext_ref[0]
    count = count_ref[frame]

    def work(slots):
        query = query_pad[...]
        dcontext = dcontext_pad[...]
        query_t = query.T
        dcontext_t = dcontext.T
        lane = lax.rem(lax.broadcasted_iota(jnp.int32, (1, 2 * TILE), 1), TILE)
        places, biases = [], []
        for j in range(slots):
            place = tiles_ref[frame, j]
            seen = jnp.where(j < count, fill_ref[place], 0)
            places.append(place)
            biases.append(jnp.where(lane < seen, 0.0, -1e30))
        for j in range(slots):
            columns = slice(j * 2 * TILE, (j + 1) * 2 * TILE)
            scores_scr[:, columns] = dot_nt(query, pair_keys[places[j]]) + biases[j]
            dattention_scr[:, columns] = dot_nt(dcontext, pair_values[places[j]])
        for start in range(0, padded, 16):
            rows = slice(start, start + 16)
            scores = [scores_scr[rows, j * 2 * TILE : (j + 1) * 2 * TILE] for j in range(slots)]
            highest = functools.reduce(jnp.maximum, scores)
            highest = per_head(jnp.max, highest[:, :TILE], highest[:, TILE:])
            exponent = [jnp.exp(part - highest) for part in scores]
            total = functools.reduce(jnp.add, exponent)
            inverse = 1.0 / per_head(jnp.sum, total[:, :TILE], total[:, TILE:])
            attention = [part * inverse for part in exponent]
            dattention = [
                dattention_scr[rows, j * 2 * TILE : (j + 1) * 2 * TILE] for j in range(slots)
            ]
            weighed = functools.reduce(
                jnp.add, [a * b for a, b in zip(attention, dattention)]
            )
            weighed = per_head(jnp.sum, weighed[:, :TILE], weighed[:, TILE:])
            for j in range(slots):
                columns = slice(j * 2 * TILE, (j + 1) * 2 * TILE)
                low_scr[rows, columns] = attention[j].astype(jnp.bfloat16)
                dscores_scr[rows, columns] = (
                    attention[j] * (dattention[j] - weighed)
                ).astype(jnp.bfloat16)
        context = jnp.zeros((padded, width), jnp.float32)
        dquery = jnp.zeros((padded, width), jnp.float32)
        for j in range(slots):
            columns = slice(j * 2 * TILE, (j + 1) * 2 * TILE)
            low, dscores = low_scr[:, columns], dscores_scr[:, columns]
            context += dot_nn(low, pair_values[places[j]])
            dquery += dot_nn(dscores, pair_keys[places[j]])
            sum_keys[places[j]] += dot_nn(query_t, dscores)
            sum_values[places[j]] += dot_nn(dcontext_t, low)
        context_ref[0] = context[:patch].astype(context_ref.dtype)
        dquery_ref[0] = (dquery[:patch] * scale).astype(dquery_ref.dtype)

    least = 0
    for slots in sorted({min(size, listed) for size in SIZES} | {listed}):
        pl.when((count > least) & (count <= slots))(functools.partial(work, slots))
        least = slots

    @pl.when(frame == pl.num_programs(1) - 1)
    def _():
        for total, target in ((sum_keys, dkeys_ref), (sum_values, dvalues_ref)):
            for tile in range(window):
                columns = slice(tile * TILE, (tile + 1) * TILE)
                target[:half, columns] = total[tile, :half, :TILE].astype(target.dtype)
                target[half:, columns] = total[tile, half:, TILE:].astype(target.dtype)


def attend(local_block, count_block, fill_window, query, dcontext, key_window, value_window):
    frames, patch, width = query.shape
    slots = key_window.shape[0]
    window = slots // TILE
    listed = local_block.shape[1]
    pair = 2 * TILE // 2
    padded = -(-patch // 16) * 16
    frame_spec = pl.BlockSpec((1, patch, pair), lambda p, f, *_: (f, 0, p))
    window_spec = pl.BlockSpec((slots, pair), lambda p, f, *_: (0, p))
    sums_spec = pl.BlockSpec((pair, slots), lambda p, f, *_: (p, 0))
    work = frames * patch * width * listed * TILE
    return pl.pallas_call(
        attention_kernel,
        grid_spec=pltpu.PrefetchScalarGridSpec(
            num_scalar_prefetch=3,
            grid=(width // pair, frames),
            in_specs=[frame_spec, frame_spec, window_spec, window_spec],
            out_specs=[frame_spec, frame_spec, sums_spec, sums_spec],
            scratch_shapes=[
                pltpu.VMEM((window, 2 * TILE, pair), jnp.bfloat16),
                pltpu.VMEM((window, 2 * TILE, pair), jnp.bfloat16),
                pltpu.VMEM((window, pair, 2 * TILE), jnp.float32),
                pltpu.VMEM((window, pair, 2 * TILE), jnp.float32),
                pltpu.VMEM((padded, pair), jnp.bfloat16),
                pltpu.VMEM((padded, pair), jnp.bfloat16),
                pltpu.VMEM((padded, listed * 2 * TILE), jnp.float32),
                pltpu.VMEM((padded, listed * 2 * TILE), jnp.float32),
                pltpu.VMEM((padded, listed * 2 * TILE), jnp.bfloat16),
                pltpu.VMEM((padded, listed * 2 * TILE), jnp.bfloat16),
            ],
        ),
        out_shape=[
            jax.ShapeDtypeStruct(query.shape, jnp.bfloat16),
            jax.ShapeDtypeStruct(query.shape, jnp.bfloat16),
            jax.ShapeDtypeStruct((width, slots), jnp.bfloat16),
            jax.ShapeDtypeStruct((width, slots), jnp.bfloat16),
        ],
        compiler_params=pltpu.CompilerParams(vmem_limit_bytes=40 * 1024 * 1024),
        cost_estimate=pl.CostEstimate(
            flops=48 * work,
            bytes_accessed=8 * frames * patch * width + 8 * slots * width,
            transcendentals=work // 64,
        ),
        name="attend",
    )(local_block, count_block, fill_window, query, dcontext, key_window, value_window)


def per_device(
    video,
    audio,
    w_query,
    w_key,
    w_value,
    w_out,
    grad_output,
    intersection_tiles,
    intersection_count,
    tile_fill,
):
    tiles_dev = tile_fill.shape[0]
    window_tiles = (2 * REACH + 1) * tiles_dev
    frames = intersection_count.shape[0]
    features = video.shape[1]
    contract_rows = (((0,), (0,)), ((), ()))
    video_normed, video_hat, video_inverse = normalize(video)
    audio_normed, audio_hat, audio_inverse = normalize(audio)
    device_index = lax.axis_index(("frame", "audio"))
    fill_rows = jnp.pad(tile_fill[None, :], ((0, 7), (0, TILE - tiles_dev)))
    normed_window, fill_window = gather_halo(audio_normed, fill_rows)
    normed_window = normed_window.reshape(-1, features)
    fill_window = fill_window[:, 0, :tiles_dev].reshape(-1)
    local_block = jnp.clip(
        intersection_tiles - (device_index - REACH) * tiles_dev, 0, window_tiles - 1
    )
    query = dot_nn(video_normed, w_query).astype(jnp.bfloat16)
    dcontext = dot_nt(grad_output, w_out).astype(jnp.bfloat16)
    key_window = dot_nn(normed_window, w_key).astype(jnp.bfloat16)
    value_window = dot_nn(normed_window, w_value).astype(jnp.bfloat16)
    context, dquery, dkeys, dvalues = attend(
        local_block,
        intersection_count,
        fill_window,
        query.reshape(frames, -1, features),
        dcontext.reshape(frames, -1, features),
        key_window,
        value_window,
    )
    context = context.reshape(-1, features)
    dquery = dquery.reshape(-1, features)
    window_rows = (((0,), (1,)), ((), ()))
    partial_sums = []
    for left, right, dims in (
        (video_normed, dquery, contract_rows),
        (normed_window, dkeys, window_rows),
        (normed_window, dvalues, window_rows),
        (context, grad_output, contract_rows),
    ):
        product = lax.dot_general(left, right, dims, preferred_element_type=jnp.float32)
        partial_sums += [product[:, i : i + LANES] for i in range(0, features, LANES)]
    dnormed_window = lax.dot_general(
        dkeys, w_key, (((0,), (1,)), ((), ())), preferred_element_type=jnp.float32
    ) + lax.dot_general(
        dvalues, w_value, (((0,), (1,)), ((), ())), preferred_element_type=jnp.float32
    )
    dnormed_window = dnormed_window.reshape(2 * REACH + 1, -1, features)
    back = jnp.concatenate([dnormed_window[:REACH], dnormed_window[REACH + 1 :]])
    total, returned = sum_devices(jnp.concatenate(partial_sums), back.astype(jnp.bfloat16))
    daudio_normed = dnormed_window[REACH] + jnp.sum(returned.astype(jnp.float32), axis=0)
    grad_audio = normalize_back(daudio_normed, audio_hat, audio_inverse).astype(jnp.bfloat16)
    attended = dot_nn(context, w_out)
    output = (video.astype(jnp.float32) + attended).astype(jnp.bfloat16)
    dvideo_normed = dot_nt(dquery, w_query)
    grad_video = (
        grad_output.astype(jnp.float32) + normalize_back(dvideo_normed, video_hat, video_inverse)
    ).astype(jnp.bfloat16)
    total = total.reshape(4, features // LANES, features, LANES).swapaxes(1, 2)
    total = total.reshape(4, features, features).astype(jnp.float32)
    return (output, grad_video, grad_audio, total[0], total[1], total[2], total[3])


def solution(mesh):
    in_specs = (
        P(("frame", "audio"), None),
        P(("frame", "audio"), None),
        P(),
        P(),
        P(),
        P(),
        P(("frame", "audio"), None),
        P(("frame", "audio"), None),
        P(("frame", "audio")),
        P(("frame", "audio")),
    )
    out_specs = (
        P(("frame", "audio"), None),
        P(("frame", "audio"), None),
        P(("frame", "audio"), None),
        P(),
        P(),
        P(),
        P(),
    )
    return jax.shard_map(
        per_device, mesh=mesh, in_specs=in_specs, out_specs=out_specs, check_vma=False
    )
```

```python
import functools
import math

import jax
import jax.numpy as jnp
from jax import lax
from jax.experimental import pallas as pl
from jax.experimental.pallas import tpu as pltpu
from jax.sharding import PartitionSpec as P

HEADS = 12
TILE = 128
REACH = 2
STREAMS = 3
MESH = pl.DeviceIdType.MESH
SIZES = (2, 4, 6, 8)


def neighbour(distance):
    inner, total = lax.axis_size("audio"), lax.axis_size("audio") * lax.axis_size("frame")
    index = lax.axis_index("frame") * inner + lax.axis_index("audio") + distance
    exists = (index >= 0) & (index < total)
    index = lax.rem(index + total, total)
    return (index // inner, lax.rem(index, inner)), exists


def other_offsets():
    return [offset for offset in range(-REACH, REACH + 1) if offset != 0]


def greet_neighbours(barrier, others=0):
    for offset in other_offsets():
        device, _ = neighbour(offset)
        pl.semaphore_signal(barrier, inc=1, device_id=device, device_id_type=MESH)
    pl.semaphore_wait(barrier, 2 * REACH + others)


def tile_rows(rows):
    return max(part for part in range(16, min(rows, 256) + 1, 16) if rows % part == 0)


def halo_kernel(
    rows_ref,
    fill_ref,
    normed_ref,
    grad_ref,
    w_query_ref,
    w_out_ref,
    window_ref,
    fills_ref,
    query_ref,
    dcontext_ref,
    send_sems,
    recv_sems,
):
    greet_neighbours(pltpu.get_barrier_semaphore())

    def copies(offset):
        device, exists = neighbour(offset)
        place = REACH - offset
        return exists, [
            pltpu.make_async_remote_copy(
                src_ref=source,
                dst_ref=target.at[place],
                send_sem=send_sems.at[i, place],
                recv_sem=recv_sems.at[i, place],
                device_id=device,
                device_id_type=MESH,
            )
            for i, (source, target) in enumerate(((rows_ref, window_ref), (fill_ref, fills_ref)))
        ]

    for offset in other_offsets():
        exists, pair = copies(offset)

        @pl.when(exists)
        def _():
            for copy in pair:
                copy.start()

    window_ref[REACH] = rows_ref[...]
    fills_ref[REACH] = fill_ref[...]
    for offset in other_offsets():
        _, exists = neighbour(-offset)
        place = REACH - offset

        @pl.when(jnp.logical_not(exists))
        def _():
            window_ref[place] = jnp.zeros(rows_ref.shape, rows_ref.dtype)
            fills_ref[place] = jnp.zeros(fill_ref.shape, fill_ref.dtype)

    part = tile_rows(normed_ref.shape[0])

    def project(i, carry):
        at = pl.ds(pl.multiple_of(i * part, 16), part)
        query_ref[at, :] = dot_nn(normed_ref[at, :], w_query_ref[...]).astype(query_ref.dtype)
        dcontext_ref[at, :] = dot_nt(grad_ref[at, :], w_out_ref[...]).astype(dcontext_ref.dtype)
        return carry

    lax.fori_loop(0, normed_ref.shape[0] // part, project, 0)
    for offset in other_offsets():
        exists, pair = copies(offset)
        _, comes = neighbour(-offset)

        @pl.when(exists)
        def _():
            for copy in pair:
                copy.wait_send()

        @pl.when(comes)
        def _():
            for copy in pair:
                copy.wait_recv()


def gather_halo(rows, fill, normed, grad, w_query, w_out):
    vmem = pl.BlockSpec(memory_space=pltpu.VMEM)
    spread = 2 * REACH + 1
    return pl.pallas_call(
        halo_kernel,
        in_specs=[vmem] * 6,
        out_specs=[vmem] * 4,
        out_shape=[
            jax.ShapeDtypeStruct((spread, *rows.shape), rows.dtype),
            jax.ShapeDtypeStruct((spread, *fill.shape), fill.dtype),
            jax.ShapeDtypeStruct(normed.shape, normed.dtype),
            jax.ShapeDtypeStruct(grad.shape, grad.dtype),
        ],
        scratch_shapes=[
            pltpu.SemaphoreType.DMA((2, spread)),
            pltpu.SemaphoreType.DMA((2, spread)),
        ],
        compiler_params=pltpu.CompilerParams(
            collective_id=1, has_side_effects=True, vmem_limit_bytes=32 * 1024 * 1024
        ),
        name="gather_halo",
    )(rows, fill, normed, grad, w_query, w_out)


def partner(axis, bit):
    me = lax.axis_index(axis)
    mine = lax.rem(me // (1 << bit), 2)
    other = me + (1 << bit) * (1 - 2 * mine)
    if axis == "frame":
        return (other, lax.axis_index("audio")), mine
    return (lax.axis_index("frame"), other), mine


def sum_kernel(
    bits,
    sums_refs,
    back_ref,
    context_ref,
    dquery_ref,
    video_ref,
    grad_ref,
    w_out_ref,
    w_query_ref,
    total_ref,
    returned_ref,
    output_ref,
    grad_video_ref,
    whole_recv,
    running,
    outgoing,
    incoming_low,
    incoming,
    first_send,
    first_recv,
    send_sems,
    recv_sems,
    gather_send,
    gather_recv,
    back_send,
    back_recv,
):
    steps = len(bits)
    depth, features = total_ref.shape[1:]
    half = features // 2
    share = depth // len(sums_refs)
    middle = list(bits[1:-1])
    orders = []
    for stream in range(STREAMS):
        turn = stream % len(middle)
        orders.append([bits[0], *middle[turn:], *middle[:turn], bits[-1]])
    barrier = pltpu.get_barrier_semaphore()
    for axis, bit in bits:
        device, _ = partner(axis, bit)
        pl.semaphore_signal(barrier, inc=1, device_id=device, device_id_type=MESH)
    greet_neighbours(barrier, steps)

    def remote(source, target, send_sem, recv_sem, device):
        return pltpu.make_async_remote_copy(
            src_ref=source,
            dst_ref=target,
            send_sem=send_sem,
            recv_sem=recv_sem,
            device_id=device,
            device_id_type=MESH,
        )

    def aligned(row):
        return pl.multiple_of(row, 16)

    def by_rows(rows, body):
        chunk = min(rows, 64)

        def step(i, carry):
            body(i * chunk, chunk)
            return carry

        lax.fori_loop(0, rows // chunk, step, 0)

    def columns(mine):
        return pl.ds(pl.multiple_of(mine * half, 128), half)

    bases = [0] * STREAMS
    started = []

    def start_step(stream, k):
        device, mine = partner(*orders[stream][k])
        if k == 0:
            copies = [
                remote(
                    source.at[pl.ds(stream * share, share), columns(1 - mine)],
                    whole_recv.at[stream, pl.ds(i * share, share)],
                    first_send.at[stream, i],
                    first_recv.at[stream, i],
                    device,
                )
                for i, source in enumerate(sums_refs)
            ]
        else:
            rows = depth >> k
            away = bases[stream] + (1 - mine) * rows
            semaphores = (send_sems.at[stream, k], recv_sems.at[stream, k])
            if k == 1:

                def cast(i, chunk):
                    own = running[stream, pl.ds(aligned(away + i), chunk), :]
                    at = pl.ds(pl.multiple_of(i, 16), chunk)
                    outgoing[stream, at, :] = own.astype(outgoing.dtype)

                by_rows(rows, cast)
                copies = [remote(outgoing.at[stream], incoming_low.at[stream], *semaphores, device)]
            else:
                place = depth // 2 - 2 * rows
                source = running.at[stream, pl.ds(aligned(away), rows)]
                target = incoming.at[stream, pl.ds(place, rows)]
                copies = [remote(source, target, *semaphores, device)]
        for copy in copies:
            copy.start()
        return copies

    def finish_step(stream, k, copies):
        _, mine = partner(*orders[stream][k])
        for copy in copies:
            copy.wait_recv()
        if k == 0:
            for i, source in enumerate(sums_refs):

                def add(row, chunk):
                    at = pl.ds(aligned(i * share + row), chunk)
                    own = source[pl.ds(aligned(stream * share + row), chunk), columns(mine)]
                    running[stream, at, :] = own + whole_recv[stream, at, :]

                by_rows(share, add)
            return
        rows = depth >> k
        bases[stream] = bases[stream] + mine * rows
        place = 0 if k == 1 else depth // 2 - 2 * rows
        source = incoming_low if k == 1 else incoming

        def add(i, chunk):
            at = pl.ds(aligned(bases[stream] + i), chunk)
            arrived = source[stream, pl.ds(aligned(place + i), chunk), :]
            running[stream, at, :] += arrived.astype(running.dtype)

        by_rows(rows, add)

    part = tile_rows(video_ref.shape[0])
    parts = video_ref.shape[0] // part
    rounds = 2 * steps

    def work(turn):
        def rows_of(i, carry):
            at = pl.ds(pl.multiple_of(i * part, 16), part)
            video = video_ref[at, :].astype(jnp.float32)
            attended = dot_nn(context_ref[at, :], w_out_ref[...])
            output_ref[at, :] = (video + attended).astype(output_ref.dtype)
            _, video_hat, inverse = normalize(video)
            back = normalize_back(dot_nt(dquery_ref[at, :], w_query_ref[...]), video_hat, inverse)
            grad = grad_ref[at, :].astype(jnp.float32)
            grad_video_ref[at, :] = (grad + back).astype(grad_video_ref.dtype)
            return carry

        first, last = turn * parts // rounds, (turn + 1) * parts // rounds
        if last > first:
            lax.fori_loop(first, last, rows_of, 0)

    live = [start_step(stream, 0) for stream in range(STREAMS)]

    def back_copy(offset):
        device, exists = neighbour(offset)
        place = offset + REACH - (offset > 0)
        return exists, remote(
            back_ref.at[place], returned_ref.at[place], back_send.at[place], back_recv.at[place], device
        )

    for offset in other_offsets():
        exists, copy = back_copy(offset)
        pl.when(exists)(copy.start)
    for offset in other_offsets():
        _, comes = neighbour(-offset)
        place = offset + REACH - (offset > 0)

        @pl.when(jnp.logical_not(comes))
        def _():
            returned_ref[place] = jnp.zeros(returned_ref.shape[1:], returned_ref.dtype)

    for k in range(steps):
        for stream in range(STREAMS):
            finish_step(stream, k, live[stream])
            started += live[stream]
            if k + 1 < steps:
                live[stream] = start_step(stream, k + 1)
        work(k)

    kept = [partner(*orders[stream][0])[1] for stream in range(STREAMS)]

    def gather_copy(stream, k):
        device, _ = partner(*orders[stream][k])
        rows = depth >> k if k else depth
        at = total_ref.at[stream, pl.ds(aligned(bases[stream]), rows), columns(kept[stream])]
        return remote(at, at, gather_send.at[stream, k], gather_recv.at[stream, k], device)

    for stream in range(STREAMS):

        def finish(i, chunk):
            at = pl.ds(aligned(bases[stream] + i), chunk)
            own = running[stream, at, :].astype(total_ref.dtype)
            total_ref[stream, at, columns(kept[stream])] = own

        by_rows(depth >> (steps - 1), finish)
        live[stream] = gather_copy(stream, steps - 1)
        live[stream].start()
    for k in reversed(range(steps)):
        work(2 * steps - 1 - k)
        for stream in range(STREAMS):
            _, mine = partner(*orders[stream][k])
            live[stream].wait_recv()
            started.append(live[stream])
            if k > 0:
                bases[stream] = bases[stream] - mine * (depth >> k)
                live[stream] = gather_copy(stream, k - 1)
                live[stream].start()
    for copy in started:
        copy.wait_send()
    for offset in other_offsets():
        exists, copy = back_copy(offset)
        _, comes = neighbour(-offset)
        pl.when(exists)(copy.wait_send)
        pl.when(comes)(copy.wait_recv)


def sum_devices(sums, back, context, dquery, video, grad, w_out, w_query):
    bits = [
        (axis, bit)
        for axis in ("audio", "frame")
        for bit in range((lax.axis_size(axis) - 1).bit_length())
    ]
    steps = len(bits)
    rows, features = sums[0].shape
    depth = len(sums) * rows // STREAMS
    half = features // 2
    vmem = pl.BlockSpec(memory_space=pltpu.VMEM)
    return pl.pallas_call(
        functools.partial(sum_kernel, bits),
        in_specs=[[vmem] * len(sums)] + [vmem] * 7,
        out_specs=[vmem] * 4,
        out_shape=[
            jax.ShapeDtypeStruct((STREAMS, depth, features), jnp.bfloat16),
            jax.ShapeDtypeStruct(back.shape, back.dtype),
            jax.ShapeDtypeStruct(video.shape, video.dtype),
            jax.ShapeDtypeStruct(grad.shape, grad.dtype),
        ],
        scratch_shapes=[
            pltpu.VMEM((STREAMS, depth, half), jnp.float32),
            pltpu.VMEM((STREAMS, depth, half), jnp.float32),
            pltpu.VMEM((STREAMS, depth // 2, half), jnp.bfloat16),
            pltpu.VMEM((STREAMS, depth // 2, half), jnp.bfloat16),
            pltpu.VMEM((STREAMS, depth // 2, half), jnp.float32),
            pltpu.SemaphoreType.DMA((STREAMS, len(sums))),
            pltpu.SemaphoreType.DMA((STREAMS, len(sums))),
            pltpu.SemaphoreType.DMA((STREAMS, steps)),
            pltpu.SemaphoreType.DMA((STREAMS, steps)),
            pltpu.SemaphoreType.DMA((STREAMS, steps)),
            pltpu.SemaphoreType.DMA((STREAMS, steps)),
            pltpu.SemaphoreType.DMA((2 * REACH,)),
            pltpu.SemaphoreType.DMA((2 * REACH,)),
        ],
        compiler_params=pltpu.CompilerParams(
            collective_id=2, has_side_effects=True, vmem_limit_bytes=52 * 1024 * 1024
        ),
        name="sum_devices",
    )(sums, back, context, dquery, video, grad, w_out, w_query)


def normalize(row_block):
    centred = row_block.astype(jnp.float32)
    centred = centred - jnp.mean(centred, axis=-1, keepdims=True)
    inverse = lax.rsqrt(jnp.mean(centred * centred, axis=-1, keepdims=True) + 1e-05)
    normed_hat = centred * inverse
    return (normed_hat.astype(jnp.bfloat16), normed_hat, inverse)


def normalize_back(gradient, normed_hat, inverse):
    first = jnp.mean(gradient, axis=-1, keepdims=True)
    second = jnp.mean(gradient * normed_hat, axis=-1, keepdims=True)
    return inverse * (gradient - first - normed_hat * second)


def dot_nt(left, right):
    return lax.dot_general(left, right, (((1,), (1,)), ((), ())), preferred_element_type=jnp.float32)


def dot_nn(left, right):
    return jnp.dot(left, right, preferred_element_type=jnp.float32)


def per_head(reduced, low, high):
    rows = low.shape[0]
    return jnp.concatenate(
        [
            jnp.broadcast_to(reduced(low, axis=1, keepdims=True), (rows, TILE)),
            jnp.broadcast_to(reduced(high, axis=1, keepdims=True), (rows, TILE)),
        ],
        axis=1,
    )


def attention_kernel(
    tiles_ref,
    count_ref,
    fill_ref,
    query_ref,
    dcontext_ref,
    keys_ref,
    values_ref,
    context_ref,
    dquery_ref,
    dkeys_ref,
    dvalues_ref,
    pair_keys,
    pair_values,
    sum_keys,
    sum_values,
    query_pad,
    dcontext_pad,
    scores_scr,
    dattention_scr,
    low_scr,
    dscores_scr,
):
    frame = pl.program_id(1)
    patch = query_ref.shape[1]
    padded, width = query_pad.shape
    half = width // 2
    listed = tiles_ref.shape[1]
    window = pair_keys.shape[0]
    scale = 1.0 / math.sqrt(half)

    @pl.when(frame == 0)
    def _():
        first = lax.broadcasted_iota(jnp.int32, (TILE, width), 1) < half
        for tile in range(window):
            for source, target in ((keys_ref, pair_keys), (values_ref, pair_values)):
                block = source[tile * TILE : (tile + 1) * TILE, :]
                zero = jnp.zeros_like(block)
                target[tile, :TILE, :] = jnp.where(first, block, zero)
                target[tile, TILE:, :] = jnp.where(first, zero, block)
        sum_keys[...] = jnp.zeros_like(sum_keys)
        sum_values[...] = jnp.zeros_like(sum_values)
        for pad in (query_pad, dcontext_pad):
            pad[padded - 16 :, :] = jnp.zeros((16, width), pad.dtype)

    query_pad[:patch, :] = query_ref[0] * jnp.asarray(scale, query_ref.dtype)
    dcontext_pad[:patch, :] = dcontext_ref[0]
    count = count_ref[frame]

    def work(slots):
        query = query_pad[...]
        dcontext = dcontext_pad[...]
        query_t = query.T
        dcontext_t = dcontext.T
        lane = lax.rem(lax.broadcasted_iota(jnp.int32, (1, 2 * TILE), 1), TILE)
        places, biases = [], []
        for j in range(slots):
            place = tiles_ref[frame, j]
            seen = jnp.where(j < count, fill_ref[place], 0)
            places.append(place)
            biases.append(jnp.where(lane < seen, 0.0, -1e30))
        for j in range(slots):
            columns = slice(j * 2 * TILE, (j + 1) * 2 * TILE)
            scores_scr[:, columns] = dot_nt(query, pair_keys[places[j]]) + biases[j]
            dattention_scr[:, columns] = dot_nt(dcontext, pair_values[places[j]])
        for start in range(0, padded, 16):
            rows = slice(start, start + 16)
            scores = [scores_scr[rows, j * 2 * TILE : (j + 1) * 2 * TILE] for j in range(slots)]
            highest = functools.reduce(jnp.maximum, scores)
            highest = per_head(jnp.max, highest[:, :TILE], highest[:, TILE:])
            exponent = [jnp.exp(part - highest) for part in scores]
            total = functools.reduce(jnp.add, exponent)
            inverse = 1.0 / per_head(jnp.sum, total[:, :TILE], total[:, TILE:])
            attention = [part * inverse for part in exponent]
            dattention = [
                dattention_scr[rows, j * 2 * TILE : (j + 1) * 2 * TILE] for j in range(slots)
            ]
            weighed = functools.reduce(
                jnp.add, [a * b for a, b in zip(attention, dattention)]
            )
            weighed = per_head(jnp.sum, weighed[:, :TILE], weighed[:, TILE:])
            for j in range(slots):
                columns = slice(j * 2 * TILE, (j + 1) * 2 * TILE)
                low_scr[rows, columns] = attention[j].astype(jnp.bfloat16)
                dscores_scr[rows, columns] = (
                    attention[j] * (dattention[j] - weighed)
                ).astype(jnp.bfloat16)
        context = jnp.zeros((padded, width), jnp.float32)
        dquery = jnp.zeros((padded, width), jnp.float32)
        for j in range(slots):
            columns = slice(j * 2 * TILE, (j + 1) * 2 * TILE)
            low, dscores = low_scr[:, columns], dscores_scr[:, columns]
            context += dot_nn(low, pair_values[places[j]])
            dquery += dot_nn(dscores, pair_keys[places[j]])
            sum_keys[places[j]] += dot_nn(query_t, dscores)
            sum_values[places[j]] += dot_nn(dcontext_t, low)
        context_ref[0] = context[:patch].astype(context_ref.dtype)
        dquery_ref[0] = (dquery[:patch] * scale).astype(dquery_ref.dtype)

    least = 0
    for slots in sorted({min(size, listed) for size in SIZES} | {listed}):
        pl.when((count > least) & (count <= slots))(functools.partial(work, slots))
        least = slots

    @pl.when(frame == pl.num_programs(1) - 1)
    def _():
        for total, target in ((sum_keys, dkeys_ref), (sum_values, dvalues_ref)):
            for tile in range(window):
                columns = slice(tile * TILE, (tile + 1) * TILE)
                target[:half, columns] = total[tile, :half, :TILE].astype(target.dtype)
                target[half:, columns] = total[tile, half:, TILE:].astype(target.dtype)


def attend(local_block, count_block, fill_window, query, dcontext, key_window, value_window):
    frames, patch, width = query.shape
    slots = key_window.shape[0]
    window = slots // TILE
    listed = local_block.shape[1]
    pair = 2 * TILE // 2
    padded = -(-patch // 16) * 16
    frame_spec = pl.BlockSpec((1, patch, pair), lambda p, f, *_: (f, 0, p))
    window_spec = pl.BlockSpec((slots, pair), lambda p, f, *_: (0, p))
    sums_spec = pl.BlockSpec((pair, slots), lambda p, f, *_: (p, 0))
    work = frames * patch * width * listed * TILE
    return pl.pallas_call(
        attention_kernel,
        grid_spec=pltpu.PrefetchScalarGridSpec(
            num_scalar_prefetch=3,
            grid=(width // pair, frames),
            in_specs=[frame_spec, frame_spec, window_spec, window_spec],
            out_specs=[frame_spec, frame_spec, sums_spec, sums_spec],
            scratch_shapes=[
                pltpu.VMEM((window, 2 * TILE, pair), jnp.bfloat16),
                pltpu.VMEM((window, 2 * TILE, pair), jnp.bfloat16),
                pltpu.VMEM((window, pair, 2 * TILE), jnp.float32),
                pltpu.VMEM((window, pair, 2 * TILE), jnp.float32),
                pltpu.VMEM((padded, pair), jnp.bfloat16),
                pltpu.VMEM((padded, pair), jnp.bfloat16),
                pltpu.VMEM((padded, listed * 2 * TILE), jnp.float32),
                pltpu.VMEM((padded, listed * 2 * TILE), jnp.float32),
                pltpu.VMEM((padded, listed * 2 * TILE), jnp.bfloat16),
                pltpu.VMEM((padded, listed * 2 * TILE), jnp.bfloat16),
            ],
        ),
        out_shape=[
            jax.ShapeDtypeStruct(query.shape, jnp.bfloat16),
            jax.ShapeDtypeStruct(query.shape, jnp.bfloat16),
            jax.ShapeDtypeStruct((width, slots), jnp.bfloat16),
            jax.ShapeDtypeStruct((width, slots), jnp.bfloat16),
        ],
        compiler_params=pltpu.CompilerParams(vmem_limit_bytes=40 * 1024 * 1024),
        cost_estimate=pl.CostEstimate(
            flops=48 * work,
            bytes_accessed=8 * frames * patch * width + 8 * slots * width,
            transcendentals=work // 64,
        ),
        name="attend",
    )(local_block, count_block, fill_window, query, dcontext, key_window, value_window)


def per_device(
    video,
    audio,
    w_query,
    w_key,
    w_value,
    w_out,
    grad_output,
    intersection_tiles,
    intersection_count,
    tile_fill,
):
    tiles_dev = tile_fill.shape[0]
    window_tiles = (2 * REACH + 1) * tiles_dev
    frames = intersection_count.shape[0]
    features = video.shape[1]
    contract_rows = (((0,), (0,)), ((), ()))
    video_normed, _, _ = normalize(video)
    audio_normed, audio_hat, audio_inverse = normalize(audio)
    device_index = lax.axis_index(("frame", "audio"))
    fill_rows = jnp.pad(tile_fill[None, :], ((0, 7), (0, TILE - tiles_dev)))
    normed_window, fill_window, query, dcontext = gather_halo(
        audio_normed, fill_rows, video_normed, grad_output, w_query, w_out
    )
    normed_window = normed_window.reshape(-1, features)
    fill_window = fill_window[:, 0, :tiles_dev].reshape(-1)
    local_block = jnp.clip(
        intersection_tiles - (device_index - REACH) * tiles_dev, 0, window_tiles - 1
    )
    key_window = dot_nn(normed_window, w_key).astype(jnp.bfloat16)
    value_window = dot_nn(normed_window, w_value).astype(jnp.bfloat16)
    context, dquery, dkeys, dvalues = attend(
        local_block,
        intersection_count,
        fill_window,
        query.reshape(frames, -1, features),
        dcontext.reshape(frames, -1, features),
        key_window,
        value_window,
    )
    context = context.reshape(-1, features)
    dquery = dquery.reshape(-1, features)
    window_rows = (((0,), (1,)), ((), ()))
    partial_sums = [
        lax.dot_general(left, right, dims, preferred_element_type=jnp.float32)
        for left, right, dims in (
            (video_normed, dquery, contract_rows),
            (normed_window, dkeys, window_rows),
            (normed_window, dvalues, window_rows),
            (context, grad_output, contract_rows),
        )
    ]
    dnormed_window = lax.dot_general(
        dkeys, w_key, (((0,), (1,)), ((), ())), preferred_element_type=jnp.float32
    ) + lax.dot_general(
        dvalues, w_value, (((0,), (1,)), ((), ())), preferred_element_type=jnp.float32
    )
    dnormed_window = dnormed_window.reshape(2 * REACH + 1, -1, features)
    back = jnp.concatenate([dnormed_window[:REACH], dnormed_window[REACH + 1 :]])
    total, returned, output, grad_video = sum_devices(
        partial_sums,
        back.astype(jnp.bfloat16),
        context,
        dquery,
        video,
        grad_output,
        w_out,
        w_query,
    )
    daudio_normed = dnormed_window[REACH] + jnp.sum(returned.astype(jnp.float32), axis=0)
    grad_audio = normalize_back(daudio_normed, audio_hat, audio_inverse).astype(jnp.bfloat16)
    total = total.reshape(STREAMS, len(partial_sums), -1, features).astype(jnp.float32)
    total = [total[:, i].reshape(-1, features) for i in range(len(partial_sums))]
    return (output, grad_video, grad_audio, total[0], total[1], total[2], total[3])


def solution(mesh):
    in_specs = (
        P(("frame", "audio"), None),
        P(("frame", "audio"), None),
        P(),
        P(),
        P(),
        P(),
        P(("frame", "audio"), None),
        P(("frame", "audio"), None),
        P(("frame", "audio")),
        P(("frame", "audio")),
    )
    out_specs = (
        P(("frame", "audio"), None),
        P(("frame", "audio"), None),
        P(("frame", "audio"), None),
        P(),
        P(),
        P(),
        P(),
    )
    return jax.shard_map(
        per_device, mesh=mesh, in_specs=in_specs, out_specs=out_specs, check_vma=False
    )
```

```python
import functools
import math

import jax
import jax.numpy as jnp
from jax import lax
from jax.experimental import pallas as pl
from jax.experimental.pallas import tpu as pltpu
from jax.sharding import PartitionSpec as P

HEADS = 12
TILE = 128
REACH = 2
STREAMS = 3
MESH = pl.DeviceIdType.MESH
SIZES = (1, 2, 3, 4, 5, 6, 7, 8)


def neighbour(distance):
    inner, total = lax.axis_size("audio"), lax.axis_size("audio") * lax.axis_size("frame")
    index = lax.axis_index("frame") * inner + lax.axis_index("audio") + distance
    exists = (index >= 0) & (index < total)
    index = lax.rem(index + total, total)
    return (index // inner, lax.rem(index, inner)), exists


def other_offsets():
    return [offset for offset in range(-REACH, REACH + 1) if offset != 0]


def greet_neighbours(barrier, others=0):
    for offset in other_offsets():
        device, _ = neighbour(offset)
        pl.semaphore_signal(barrier, inc=1, device_id=device, device_id_type=MESH)
    pl.semaphore_wait(barrier, 2 * REACH + others)


def tile_rows(rows):
    return max(part for part in range(16, min(rows, 256) + 1, 16) if rows % part == 0)


def halo_kernel(
    rows_ref,
    fill_ref,
    normed_ref,
    grad_ref,
    w_query_ref,
    w_out_ref,
    window_ref,
    fills_ref,
    query_ref,
    dcontext_ref,
    send_sems,
    recv_sems,
):
    greet_neighbours(pltpu.get_barrier_semaphore())

    def copies(offset):
        device, exists = neighbour(offset)
        place = REACH - offset
        return exists, [
            pltpu.make_async_remote_copy(
                src_ref=source,
                dst_ref=target.at[place],
                send_sem=send_sems.at[i, place],
                recv_sem=recv_sems.at[i, place],
                device_id=device,
                device_id_type=MESH,
            )
            for i, (source, target) in enumerate(((rows_ref, window_ref), (fill_ref, fills_ref)))
        ]

    for offset in other_offsets():
        exists, pair = copies(offset)

        @pl.when(exists)
        def _():
            for copy in pair:
                copy.start()

    window_ref[REACH] = rows_ref[...]
    fills_ref[REACH] = fill_ref[...]
    for offset in other_offsets():
        _, exists = neighbour(-offset)
        place = REACH - offset

        @pl.when(jnp.logical_not(exists))
        def _():
            window_ref[place] = jnp.zeros(rows_ref.shape, rows_ref.dtype)
            fills_ref[place] = jnp.zeros(fill_ref.shape, fill_ref.dtype)

    frames, patch = query_ref.shape[:2]
    for frame in range(frames):
        at = slice(frame * patch, (frame + 1) * patch)
        query_ref[frame] = dot_nn(normed_ref[at, :], w_query_ref[...]).astype(query_ref.dtype)
        dcontext_ref[frame] = dot_nt(grad_ref[at, :], w_out_ref[...]).astype(dcontext_ref.dtype)

    for offset in other_offsets():
        exists, pair = copies(offset)
        _, comes = neighbour(-offset)

        @pl.when(exists)
        def _():
            for copy in pair:
                copy.wait_send()

        @pl.when(comes)
        def _():
            for copy in pair:
                copy.wait_recv()


def gather_halo(rows, fill, normed, grad, w_query, w_out, frames):
    vmem = pl.BlockSpec(memory_space=pltpu.VMEM)
    spread = 2 * REACH + 1
    return pl.pallas_call(
        halo_kernel,
        in_specs=[vmem] * 6,
        out_specs=[vmem] * 4,
        out_shape=[
            jax.ShapeDtypeStruct((spread, *rows.shape), rows.dtype),
            jax.ShapeDtypeStruct((spread, *fill.shape), fill.dtype),
            jax.ShapeDtypeStruct((frames, normed.shape[0] // frames, normed.shape[1]), normed.dtype),
            jax.ShapeDtypeStruct((frames, grad.shape[0] // frames, grad.shape[1]), grad.dtype),
        ],
        scratch_shapes=[
            pltpu.SemaphoreType.DMA((2, spread)),
            pltpu.SemaphoreType.DMA((2, spread)),
        ],
        compiler_params=pltpu.CompilerParams(
            collective_id=1, has_side_effects=True, vmem_limit_bytes=32 * 1024 * 1024
        ),
        name="gather_halo",
    )(rows, fill, normed, grad, w_query, w_out)


def partner(axis, bit):
    me = lax.axis_index(axis)
    mine = lax.rem(me // (1 << bit), 2)
    other = me + (1 << bit) * (1 - 2 * mine)
    if axis == "frame":
        return (other, lax.axis_index("audio")), mine
    return (lax.axis_index("frame"), other), mine


def sum_kernel(
    bits,
    sums_refs,
    back_ref,
    context_ref,
    dquery_ref,
    video_ref,
    grad_ref,
    w_out_ref,
    w_query_ref,
    total_ref,
    returned_ref,
    output_ref,
    grad_video_ref,
    whole_recv,
    running,
    outgoing,
    incoming_low,
    incoming,
    first_send,
    first_recv,
    send_sems,
    recv_sems,
    gather_send,
    gather_recv,
    back_send,
    back_recv,
):
    steps = len(bits)
    depth, features = total_ref.shape[1:]
    half = features // 2
    share = depth // len(sums_refs)
    middle = list(bits[1:-1])
    orders = []
    for stream in range(STREAMS):
        turn = stream % len(middle)
        orders.append([bits[0], *middle[turn:], *middle[:turn], bits[-1]])
    barrier = pltpu.get_barrier_semaphore()
    for axis, bit in bits:
        device, _ = partner(axis, bit)
        pl.semaphore_signal(barrier, inc=1, device_id=device, device_id_type=MESH)
    greet_neighbours(barrier, steps)

    def remote(source, target, send_sem, recv_sem, device):
        return pltpu.make_async_remote_copy(
            src_ref=source,
            dst_ref=target,
            send_sem=send_sem,
            recv_sem=recv_sem,
            device_id=device,
            device_id_type=MESH,
        )

    def aligned(row):
        return pl.multiple_of(row, 16)

    def by_rows(rows, body):
        chunk = min(rows, 64)

        def step(i, carry):
            body(i * chunk, chunk)
            return carry

        lax.fori_loop(0, rows // chunk, step, 0)

    def columns(mine):
        return pl.ds(pl.multiple_of(mine * half, 128), half)

    bases = [0] * STREAMS
    started = []

    def start_step(stream, k):
        device, mine = partner(*orders[stream][k])
        if k == 0:
            copies = [
                remote(
                    source.at[pl.ds(stream * share, share), columns(1 - mine)],
                    whole_recv.at[stream, pl.ds(i * share, share)],
                    first_send.at[stream, i],
                    first_recv.at[stream, i],
                    device,
                )
                for i, source in enumerate(sums_refs)
            ]
        else:
            rows = depth >> k
            away = bases[stream] + (1 - mine) * rows
            semaphores = (send_sems.at[stream, k], recv_sems.at[stream, k])
            if k == 1:

                def cast(i, chunk):
                    own = running[stream, pl.ds(aligned(away + i), chunk), :]
                    at = pl.ds(pl.multiple_of(i, 16), chunk)
                    outgoing[stream, at, :] = own.astype(outgoing.dtype)

                by_rows(rows, cast)
                copies = [remote(outgoing.at[stream], incoming_low.at[stream], *semaphores, device)]
            else:
                place = depth // 2 - 2 * rows
                source = running.at[stream, pl.ds(aligned(away), rows)]
                target = incoming.at[stream, pl.ds(place, rows)]
                copies = [remote(source, target, *semaphores, device)]
        for copy in copies:
            copy.start()
        return copies

    def finish_step(stream, k, copies):
        _, mine = partner(*orders[stream][k])
        for copy in copies:
            copy.wait_recv()
        if k == 0:
            for i, source in enumerate(sums_refs):

                def add(row, chunk):
                    at = pl.ds(aligned(i * share + row), chunk)
                    own = source[pl.ds(aligned(stream * share + row), chunk), columns(mine)]
                    running[stream, at, :] = own + whole_recv[stream, at, :]

                by_rows(share, add)
            return
        rows = depth >> k
        bases[stream] = bases[stream] + mine * rows
        place = 0 if k == 1 else depth // 2 - 2 * rows
        source = incoming_low if k == 1 else incoming

        def add(i, chunk):
            at = pl.ds(aligned(bases[stream] + i), chunk)
            arrived = source[stream, pl.ds(aligned(place + i), chunk), :]
            running[stream, at, :] += arrived.astype(running.dtype)

        by_rows(rows, add)

    part = tile_rows(video_ref.shape[0])
    parts = video_ref.shape[0] // part
    rounds = 2 * steps

    def work(turn):
        def rows_of(i, carry):
            at = pl.ds(pl.multiple_of(i * part, 16), part)
            video = video_ref[at, :].astype(jnp.float32)
            attended = dot_nn(context_ref[at, :], w_out_ref[...])
            output_ref[at, :] = (video + attended).astype(output_ref.dtype)
            _, video_hat, inverse = normalize(video)
            back = normalize_back(dot_nt(dquery_ref[at, :], w_query_ref[...]), video_hat, inverse)
            grad = grad_ref[at, :].astype(jnp.float32)
            grad_video_ref[at, :] = (grad + back).astype(grad_video_ref.dtype)
            return carry

        first, last = turn * parts // rounds, (turn + 1) * parts // rounds
        if last > first:
            lax.fori_loop(first, last, rows_of, 0)

    live = [start_step(stream, 0) for stream in range(STREAMS)]

    def back_copy(offset):
        device, exists = neighbour(offset)
        place = offset + REACH - (offset > 0)
        return exists, remote(
            back_ref.at[place], returned_ref.at[place], back_send.at[place], back_recv.at[place], device
        )

    for offset in other_offsets():
        exists, copy = back_copy(offset)
        pl.when(exists)(copy.start)
    for offset in other_offsets():
        _, comes = neighbour(-offset)
        place = offset + REACH - (offset > 0)

        @pl.when(jnp.logical_not(comes))
        def _():
            returned_ref[place] = jnp.zeros(returned_ref.shape[1:], returned_ref.dtype)

    for k in range(steps):
        for stream in range(STREAMS):
            finish_step(stream, k, live[stream])
            started += live[stream]
            if k + 1 < steps:
                live[stream] = start_step(stream, k + 1)
        work(k)

    kept = [partner(*orders[stream][0])[1] for stream in range(STREAMS)]

    def gather_copy(stream, k):
        device, _ = partner(*orders[stream][k])
        rows = depth >> k if k else depth
        at = total_ref.at[stream, pl.ds(aligned(bases[stream]), rows), columns(kept[stream])]
        return remote(at, at, gather_send.at[stream, k], gather_recv.at[stream, k], device)

    for stream in range(STREAMS):

        def finish(i, chunk):
            at = pl.ds(aligned(bases[stream] + i), chunk)
            own = running[stream, at, :].astype(total_ref.dtype)
            total_ref[stream, at, columns(kept[stream])] = own

        by_rows(depth >> (steps - 1), finish)
        live[stream] = gather_copy(stream, steps - 1)
        live[stream].start()
    for k in reversed(range(steps)):
        work(2 * steps - 1 - k)
        for stream in range(STREAMS):
            _, mine = partner(*orders[stream][k])
            live[stream].wait_recv()
            started.append(live[stream])
            if k > 0:
                bases[stream] = bases[stream] - mine * (depth >> k)
                live[stream] = gather_copy(stream, k - 1)
                live[stream].start()
    for copy in started:
        copy.wait_send()
    for offset in other_offsets():
        exists, copy = back_copy(offset)
        _, comes = neighbour(-offset)
        pl.when(exists)(copy.wait_send)
        pl.when(comes)(copy.wait_recv)


def sum_devices(sums, back, context, dquery, video, grad, w_out, w_query):
    bits = [
        (axis, bit)
        for axis in ("audio", "frame")
        for bit in range((lax.axis_size(axis) - 1).bit_length())
    ]
    steps = len(bits)
    rows, features = sums[0].shape
    depth = len(sums) * rows // STREAMS
    half = features // 2
    vmem = pl.BlockSpec(memory_space=pltpu.VMEM)
    return pl.pallas_call(
        functools.partial(sum_kernel, bits),
        in_specs=[[vmem] * len(sums)] + [vmem] * 7,
        out_specs=[vmem] * 4,
        out_shape=[
            jax.ShapeDtypeStruct((STREAMS, depth, features), jnp.bfloat16),
            jax.ShapeDtypeStruct(back.shape, back.dtype),
            jax.ShapeDtypeStruct(video.shape, video.dtype),
            jax.ShapeDtypeStruct(grad.shape, grad.dtype),
        ],
        scratch_shapes=[
            pltpu.VMEM((STREAMS, depth, half), jnp.float32),
            pltpu.VMEM((STREAMS, depth, half), jnp.float32),
            pltpu.VMEM((STREAMS, depth // 2, half), jnp.bfloat16),
            pltpu.VMEM((STREAMS, depth // 2, half), jnp.bfloat16),
            pltpu.VMEM((STREAMS, depth // 2, half), jnp.float32),
            pltpu.SemaphoreType.DMA((STREAMS, len(sums))),
            pltpu.SemaphoreType.DMA((STREAMS, len(sums))),
            pltpu.SemaphoreType.DMA((STREAMS, steps)),
            pltpu.SemaphoreType.DMA((STREAMS, steps)),
            pltpu.SemaphoreType.DMA((STREAMS, steps)),
            pltpu.SemaphoreType.DMA((STREAMS, steps)),
            pltpu.SemaphoreType.DMA((2 * REACH,)),
            pltpu.SemaphoreType.DMA((2 * REACH,)),
        ],
        compiler_params=pltpu.CompilerParams(
            collective_id=2, has_side_effects=True, vmem_limit_bytes=52 * 1024 * 1024
        ),
        name="sum_devices",
    )(sums, back, context, dquery, video, grad, w_out, w_query)


def normalize(row_block):
    centred = row_block.astype(jnp.float32)
    centred = centred - jnp.mean(centred, axis=-1, keepdims=True)
    inverse = lax.rsqrt(jnp.mean(centred * centred, axis=-1, keepdims=True) + 1e-05)
    normed_hat = centred * inverse
    return (normed_hat.astype(jnp.bfloat16), normed_hat, inverse)


def normalize_back(gradient, normed_hat, inverse):
    first = jnp.mean(gradient, axis=-1, keepdims=True)
    second = jnp.mean(gradient * normed_hat, axis=-1, keepdims=True)
    return inverse * (gradient - first - normed_hat * second)


def dot_nt(left, right):
    return lax.dot_general(left, right, (((1,), (1,)), ((), ())), preferred_element_type=jnp.float32)


def dot_nn(left, right):
    return jnp.dot(left, right, preferred_element_type=jnp.float32)


def per_head(reduced, low, high):
    rows = low.shape[0]
    return jnp.concatenate(
        [
            jnp.broadcast_to(reduced(low, axis=1, keepdims=True), (rows, TILE)),
            jnp.broadcast_to(reduced(high, axis=1, keepdims=True), (rows, TILE)),
        ],
        axis=1,
    )


def attention_kernel(
    tiles_ref,
    count_ref,
    fill_ref,
    query_ref,
    dcontext_ref,
    keys_ref,
    values_ref,
    context_ref,
    dquery_ref,
    dkeys_ref,
    dvalues_ref,
    pair_keys,
    pair_values,
    sum_keys,
    sum_values,
    query_pad,
    dcontext_pad,
    scores_scr,
    dattention_scr,
    low_scr,
    dscores_scr,
):
    frame = pl.program_id(1)
    patch = query_ref.shape[1]
    padded, width = query_pad.shape
    half = width // 2
    listed = tiles_ref.shape[1]
    window = pair_keys.shape[0]
    scale = 1.0 / math.sqrt(half)

    @pl.when(frame == 0)
    def _():
        first = lax.broadcasted_iota(jnp.int32, (TILE, width), 1) < half
        for tile in range(window):
            for source, target in ((keys_ref, pair_keys), (values_ref, pair_values)):
                block = source[tile * TILE : (tile + 1) * TILE, :]
                zero = jnp.zeros_like(block)
                target[tile, :TILE, :] = jnp.where(first, block, zero)
                target[tile, TILE:, :] = jnp.where(first, zero, block)
        sum_keys[...] = jnp.zeros_like(sum_keys)
        sum_values[...] = jnp.zeros_like(sum_values)
        for pad in (query_pad, dcontext_pad):
            pad[padded - 16 :, :] = jnp.zeros((16, width), pad.dtype)

    query_pad[:patch, :] = query_ref[0] * jnp.asarray(scale, query_ref.dtype)
    dcontext_pad[:patch, :] = dcontext_ref[0]
    count = count_ref[frame]

    def work(slots):
        query = query_pad[...]
        dcontext = dcontext_pad[...]
        query_t = query.T
        dcontext_t = dcontext.T
        lane = lax.rem(lax.broadcasted_iota(jnp.int32, (1, 2 * TILE), 1), TILE)
        places, biases = [], []
        for j in range(slots):
            place = tiles_ref[frame, j]
            seen = jnp.where(j < count, fill_ref[place], 0)
            places.append(place)
            biases.append(jnp.where(lane < seen, 0.0, -1e30))
        for j in range(slots):
            columns = slice(j * 2 * TILE, (j + 1) * 2 * TILE)
            scores_scr[:, columns] = dot_nt(query, pair_keys[places[j]]) + biases[j]
            dattention_scr[:, columns] = dot_nt(dcontext, pair_values[places[j]])
        for start in range(0, padded, 16):
            rows = slice(start, start + 16)
            scores = [scores_scr[rows, j * 2 * TILE : (j + 1) * 2 * TILE] for j in range(slots)]
            highest = functools.reduce(jnp.maximum, scores)
            highest = per_head(jnp.max, highest[:, :TILE], highest[:, TILE:])
            exponent = [jnp.exp(part - highest) for part in scores]
            total = functools.reduce(jnp.add, exponent)
            inverse = 1.0 / per_head(jnp.sum, total[:, :TILE], total[:, TILE:])
            attention = [part * inverse for part in exponent]
            dattention = [
                dattention_scr[rows, j * 2 * TILE : (j + 1) * 2 * TILE] for j in range(slots)
            ]
            weighed = functools.reduce(
                jnp.add, [a * b for a, b in zip(attention, dattention)]
            )
            weighed = per_head(jnp.sum, weighed[:, :TILE], weighed[:, TILE:])
            for j in range(slots):
                columns = slice(j * 2 * TILE, (j + 1) * 2 * TILE)
                low_scr[rows, columns] = attention[j].astype(jnp.bfloat16)
                dscores_scr[rows, columns] = (
                    attention[j] * (dattention[j] - weighed)
                ).astype(jnp.bfloat16)
        context = jnp.zeros((padded, width), jnp.float32)
        dquery = jnp.zeros((padded, width), jnp.float32)
        for j in range(slots):
            columns = slice(j * 2 * TILE, (j + 1) * 2 * TILE)
            low, dscores = low_scr[:, columns], dscores_scr[:, columns]
            context += dot_nn(low, pair_values[places[j]])
            dquery += dot_nn(dscores, pair_keys[places[j]])
            sum_keys[places[j]] += dot_nn(query_t, dscores)
            sum_values[places[j]] += dot_nn(dcontext_t, low)
        context_ref[0] = context[:patch].astype(context_ref.dtype)
        dquery_ref[0] = (dquery[:patch] * scale).astype(dquery_ref.dtype)

    least = 0
    for slots in sorted({min(size, listed) for size in SIZES} | {listed}):
        pl.when((count > least) & (count <= slots))(functools.partial(work, slots))
        least = slots

    @pl.when(frame == pl.num_programs(1) - 1)
    def _():
        for total, target in ((sum_keys, dkeys_ref), (sum_values, dvalues_ref)):
            for tile in range(window):
                columns = slice(tile * TILE, (tile + 1) * TILE)
                target[:half, columns] = total[tile, :half, :TILE].astype(target.dtype)
                target[half:, columns] = total[tile, half:, TILE:].astype(target.dtype)


def attend(local_block, count_block, fill_window, query, dcontext, key_window, value_window):
    frames, patch, width = query.shape
    slots = key_window.shape[0]
    window = slots // TILE
    listed = local_block.shape[1]
    pair = 2 * TILE // 2
    padded = -(-patch // 16) * 16
    frame_spec = pl.BlockSpec((1, patch, pair), lambda p, f, *_: (f, 0, p))
    window_spec = pl.BlockSpec((slots, pair), lambda p, f, *_: (0, p))
    sums_spec = pl.BlockSpec((pair, slots), lambda p, f, *_: (p, 0))
    work = frames * patch * width * listed * TILE
    return pl.pallas_call(
        attention_kernel,
        grid_spec=pltpu.PrefetchScalarGridSpec(
            num_scalar_prefetch=3,
            grid=(width // pair, frames),
            in_specs=[frame_spec, frame_spec, window_spec, window_spec],
            out_specs=[frame_spec, frame_spec, sums_spec, sums_spec],
            scratch_shapes=[
                pltpu.VMEM((window, 2 * TILE, pair), jnp.bfloat16),
                pltpu.VMEM((window, 2 * TILE, pair), jnp.bfloat16),
                pltpu.VMEM((window, pair, 2 * TILE), jnp.float32),
                pltpu.VMEM((window, pair, 2 * TILE), jnp.float32),
                pltpu.VMEM((padded, pair), jnp.bfloat16),
                pltpu.VMEM((padded, pair), jnp.bfloat16),
                pltpu.VMEM((padded, listed * 2 * TILE), jnp.float32),
                pltpu.VMEM((padded, listed * 2 * TILE), jnp.float32),
                pltpu.VMEM((padded, listed * 2 * TILE), jnp.bfloat16),
                pltpu.VMEM((padded, listed * 2 * TILE), jnp.bfloat16),
            ],
        ),
        out_shape=[
            jax.ShapeDtypeStruct(query.shape, jnp.bfloat16),
            jax.ShapeDtypeStruct(query.shape, jnp.bfloat16),
            jax.ShapeDtypeStruct((width, slots), jnp.bfloat16),
            jax.ShapeDtypeStruct((width, slots), jnp.bfloat16),
        ],
        compiler_params=pltpu.CompilerParams(vmem_limit_bytes=40 * 1024 * 1024),
        cost_estimate=pl.CostEstimate(
            flops=48 * work,
            bytes_accessed=8 * frames * patch * width + 8 * slots * width,
            transcendentals=work // 64,
        ),
        name="attend",
    )(local_block, count_block, fill_window, query, dcontext, key_window, value_window)


def per_device(
    video,
    audio,
    w_query,
    w_key,
    w_value,
    w_out,
    grad_output,
    intersection_tiles,
    intersection_count,
    tile_fill,
):
    tiles_dev = tile_fill.shape[0]
    window_tiles = (2 * REACH + 1) * tiles_dev
    frames = intersection_count.shape[0]
    features = video.shape[1]
    contract_rows = (((0,), (0,)), ((), ()))
    video_normed, _, _ = normalize(video)
    audio_normed, audio_hat, audio_inverse = normalize(audio)
    device_index = lax.axis_index(("frame", "audio"))
    fill_rows = jnp.pad(tile_fill[None, :], ((0, 7), (0, TILE - tiles_dev)))
    normed_window, fill_window, query, dcontext = gather_halo(
        audio_normed, fill_rows, video_normed, grad_output, w_query, w_out, frames
    )
    normed_window = normed_window.reshape(-1, features)
    fill_window = fill_window[:, 0, :tiles_dev].reshape(-1)
    local_block = jnp.clip(
        intersection_tiles - (device_index - REACH) * tiles_dev, 0, window_tiles - 1
    )
    key_window = dot_nn(normed_window, w_key).astype(jnp.bfloat16)
    value_window = dot_nn(normed_window, w_value).astype(jnp.bfloat16)
    context, dquery, dkeys, dvalues = attend(
        local_block,
        intersection_count,
        fill_window,
        query,
        dcontext,
        key_window,
        value_window,
    )
    context = context.reshape(-1, features)
    dquery = dquery.reshape(-1, features)
    window_rows = (((0,), (1,)), ((), ()))
    partial_sums = [
        lax.dot_general(left, right, dims, preferred_element_type=jnp.float32)
        for left, right, dims in (
            (video_normed, dquery, contract_rows),
            (normed_window, dkeys, window_rows),
            (normed_window, dvalues, window_rows),
            (context, grad_output, contract_rows),
        )
    ]
    dnormed_window = lax.dot_general(
        dkeys, w_key, (((0,), (1,)), ((), ())), preferred_element_type=jnp.float32
    ) + lax.dot_general(
        dvalues, w_value, (((0,), (1,)), ((), ())), preferred_element_type=jnp.float32
    )
    dnormed_window = dnormed_window.reshape(2 * REACH + 1, -1, features)
    back = jnp.concatenate([dnormed_window[:REACH], dnormed_window[REACH + 1 :]])
    total, returned, output, grad_video = sum_devices(
        partial_sums,
        back.astype(jnp.bfloat16),
        context,
        dquery,
        video,
        grad_output,
        w_out,
        w_query,
    )
    daudio_normed = dnormed_window[REACH] + jnp.sum(returned.astype(jnp.float32), axis=0)
    grad_audio = normalize_back(daudio_normed, audio_hat, audio_inverse).astype(jnp.bfloat16)
    total = total.reshape(STREAMS, len(partial_sums), -1, features).astype(jnp.float32)
    total = [total[:, i].reshape(-1, features) for i in range(len(partial_sums))]
    return (output, grad_video, grad_audio, total[0], total[1], total[2], total[3])


def solution(mesh):
    in_specs = (
        P(("frame", "audio"), None),
        P(("frame", "audio"), None),
        P(),
        P(),
        P(),
        P(),
        P(("frame", "audio"), None),
        P(("frame", "audio"), None),
        P(("frame", "audio")),
        P(("frame", "audio")),
    )
    out_specs = (
        P(("frame", "audio"), None),
        P(("frame", "audio"), None),
        P(("frame", "audio"), None),
        P(),
        P(),
        P(),
        P(),
    )
    return jax.shard_map(
        per_device, mesh=mesh, in_specs=in_specs, out_specs=out_specs, check_vma=False
    )
```
